32 devices in a mesh: row: 4 (over z), col: 2 (over y), layer: 4 (over x, core).
Axes of the slice: x: 2, y: 2, z: 4, core: 2. Of those that a mesh axis runs over, the one named last changes fastest.
Arguments:
- a_blocks: bfloat16 [256, 128, 128], P(('row', 'col', 'layer')), may hold values from -0.5 to 0.5
- a_codes: int32 [256], P(('row', 'col', 'layer')), may hold values from -1 to 47, as said below
- b_blocks: bfloat16 [512, 128, 128], P(('row', 'col', 'layer')), may hold values from -6 to 6
- b_codes: int32 [512], P(('row', 'col', 'layer')), may hold values from -1 to 23, as said below
Outputs:
- product: bfloat16 [2048, 1024], P(('row', 'layer'), 'col')
The draws below stay inside these ranges and needn't reach their ends.
Inputs may be any that keep to these rules, and one draw needn't show every extreme that they name: `a_codes`: slots that one owner receives (same o, same r and l, all q) carry distinct codes; in every group of 2 owners some owner receives 8 live slots, and every owner at least one. `b_codes`: slots that one owner receives (same o, same c and l, all q) carry distinct codes; in every group of 4 owners some owner receives 16 live slots, and every owner at least one.
All inputs are finite; a program needn't handle non-finite values.
Results may differ from the reference program's by a relative error of at most 0.001.
Values may be sent and summed in bfloat16 or wider, within the bound.
No kernel may reach another device: no remote copies, remote signals or barrier semaphores. Data moves between devices by JAX's collectives and lax.ppermute only.
A program may use at most 64 MiB of HBM per device.

```python
import jax
import jax.numpy as jnp
from jax import lax

BS = 128
RB = 4
CB = 4
KB = 6
S_A = 8
S_B = 16
N_ROW = 4
N_COL = 2
N_LAYER = 4


def group_codes(subkey, owners, slot_count, positions):
    key_full, key_rest = jax.random.split(subkey)
    full_owner = jax.random.randint(key_full, (), 0, owners)
    owner_keys = jax.random.split(key_rest, owners)

    def one_owner(owner_key, owner_index):
        key_live, key_place, key_order = jax.random.split(owner_key, 3)
        live_count = jax.random.randint(key_live, (), 1, slot_count + 1)
        live_count = jnp.where(owner_index == full_owner, slot_count, live_count)
        placed = jax.random.permutation(key_place, positions)[:slot_count]
        order_rank = jax.random.permutation(key_order, slot_count)
        return jnp.where(order_rank < live_count, placed[order_rank], -1).astype(jnp.int32)
    return jax.vmap(one_owner)(owner_keys, jnp.arange(owners))


def draw_a_codes(key, part):
    subkeys = jax.random.split(jax.random.fold_in(key, 11), N_ROW * N_LAYER)
    positions = RB * (N_ROW // N_COL) * KB
    groups = jax.vmap(lambda subkey: group_codes(subkey, N_COL, S_A, positions))(subkeys)
    per_peer = S_A // N_COL
    owner_view = groups.reshape(N_ROW, N_LAYER, N_COL, N_COL, per_peer)
    producer_view = owner_view.transpose(0, 3, 1, 2, 4)
    return producer_view.reshape(-1).astype(jnp.int32)


def draw_b_codes(key, part):
    subkeys = jax.random.split(jax.random.fold_in(key, 23), N_COL * N_LAYER)
    positions = KB * CB
    groups = jax.vmap(lambda subkey: group_codes(subkey, N_ROW, S_B, positions))(subkeys)
    per_peer = S_B // N_ROW
    owner_view = groups.reshape(N_COL, N_LAYER, N_ROW, N_ROW, per_peer)
    producer_view = owner_view.transpose(3, 0, 1, 2, 4)
    return producer_view.reshape(-1).astype(jnp.int32)


def block_levels(own_key, dims, shards, least, top_value):
    loudness, own = 1.0, jax.random.fold_in(own_key, 6)
    for dim, shards_of in shards:
        heights = jnp.exp(jax.random.uniform(jax.random.fold_in(own, dim), (shards_of,), jnp.float32, least / len(shards), top_value / len(shards)))
        loudness = loudness * jnp.repeat(heights, dims[dim] // shards_of).reshape([-1 if axis == dim else 1 for axis in range(len(dims))])
    return loudness


def noise(stream_key, shape, scale, reach, cuts=(), kind=jnp.bfloat16):
    entries = scale * jax.random.normal(stream_key, shape, jnp.float32)
    if cuts:
        entries = entries * block_levels(stream_key, shape, cuts, -0.22, 0.18)
    return jnp.clip(entries, -reach, reach).astype(kind)


def setup_inputs(seed: int = 0) -> dict:
    splits = jax.random.split(jax.random.key(seed), 5)
    a_blocks = noise(splits[0], (N_ROW * N_COL * N_LAYER * S_A, BS, BS), BS ** -0.5, 0.5, ((0, 32),))
    a_codes = draw_a_codes(jax.random.fold_in(splits[4], 71), 0)
    b_blocks = noise(splits[2], (N_ROW * N_COL * N_LAYER * S_B, BS, BS), 1.0, 6.0, ((0, 32),))
    b_codes = draw_b_codes(jax.random.fold_in(splits[4], 71), 0)
    return {"a_blocks": a_blocks, "a_codes": a_codes, "b_blocks": b_blocks, "b_codes": b_codes}


def dense_right(block_stack, block_codes):
    is_live = block_codes >= 0
    inner_of = block_codes // CB
    column_of = block_codes % CB
    inner_hit = inner_of[:, None] == jnp.arange(KB, dtype=jnp.int32)[None, :]
    column_hit = column_of[:, None] == jnp.arange(CB, dtype=jnp.int32)[None, :]
    weight = (is_live[:, None, None] & inner_hit[:, :, None] & column_hit[:, None, :]).astype(jnp.float32)
    dense_tile = jnp.einsum("skj,sxy->kxjy", weight, block_stack.astype(jnp.float32))
    return dense_tile.astype(jnp.bfloat16).reshape(KB, BS, CB * BS)


def reference(a_blocks, a_codes, b_blocks, b_codes):
    pieces = N_ROW // N_COL
    per_peer_a = S_A // N_COL
    per_peer_b = S_B // N_ROW
    a_owned = a_blocks.reshape(N_ROW, N_COL, N_LAYER, N_COL, per_peer_a, BS, BS)
    a_owned = a_owned.transpose(0, 3, 2, 1, 4, 5, 6).reshape(N_ROW, N_COL, N_LAYER, S_A, BS, BS)
    a_tags = a_codes.reshape(N_ROW, N_COL, N_LAYER, N_COL, per_peer_a)
    a_tags = a_tags.transpose(0, 3, 2, 1, 4).reshape(N_ROW, N_COL, N_LAYER, S_A)
    b_owned = b_blocks.reshape(N_ROW, N_COL, N_LAYER, N_ROW, per_peer_b, BS, BS)
    b_owned = b_owned.transpose(3, 1, 2, 0, 4, 5, 6).reshape(N_ROW, N_COL, N_LAYER, S_B, BS, BS)
    b_tags = b_codes.reshape(N_ROW, N_COL, N_LAYER, N_ROW, per_peer_b)
    b_tags = b_tags.transpose(3, 1, 2, 0, 4).reshape(N_ROW, N_COL, N_LAYER, S_B)

    def tile_product(tile_index):
        row_index = tile_index // N_COL
        col_index = tile_index % N_COL

        def visit_piece(accumulated, visit_step):
            layer_index = visit_step // N_ROW
            piece_index = visit_step % N_ROW
            owner_a = (piece_index - row_index) % N_COL
            owner_b = (piece_index - col_index) % N_ROW
            left_stack = a_owned[row_index, owner_a, layer_index]
            left_codes = a_tags[row_index, owner_a, layer_index]
            right_tile = dense_right(b_owned[owner_b, col_index, layer_index], b_tags[owner_b, col_index, layer_index])
            is_live = left_codes >= 0
            row_of = jnp.where(is_live, left_codes // (pieces * KB), 0)
            part_of = (left_codes // KB) % pieces
            inner_of = jnp.where(is_live, left_codes % KB, 0).astype(jnp.int32)
            selected = is_live & (part_of == piece_index // N_COL)
            row_hits = (row_of[:, None] == jnp.arange(RB, dtype=jnp.int32)[None, :]) & selected[:, None]
            gathered = right_tile[inner_of]
            products = jnp.einsum("axy,ayz->axz", left_stack.astype(jnp.float32), gathered.astype(jnp.float32))
            contrib = jnp.einsum("ai,axz->ixz", row_hits.astype(jnp.float32), products)
            return accumulated + contrib.reshape(RB * BS, CB * BS), None

        start_sum = jnp.zeros((RB * BS, CB * BS), jnp.float32)
        accumulated, _ = lax.scan(visit_piece, start_sum, jnp.arange(N_LAYER * N_ROW, dtype=jnp.int32))
        return accumulated.astype(jnp.bfloat16)

    tile_sums = lax.map(tile_product, jnp.arange(N_ROW * N_COL, dtype=jnp.int32))
    tile_sums = tile_sums.reshape(N_ROW, N_COL, RB * BS, CB * BS).transpose(0, 2, 1, 3)
    return tile_sums.reshape(N_ROW * RB * BS, N_COL * CB * BS)
```

```python
import functools

import jax
import jax.numpy as jnp
from jax import lax
from jax.experimental import pallas as pl
from jax.experimental.pallas import tpu as pltpu
from jax.sharding import PartitionSpec as P

RB = 4
CB = 4
KB = 6


def from_behind(block, axis, distance):
    devices = range(lax.axis_size(axis))
    route = [((i - distance) % len(devices), i) for i in devices]
    return lax.ppermute(block, axis, route)


def dense_left(block_stack, block_codes, part_index, pieces):
    block_width = block_stack.shape[1]
    is_live = block_codes >= 0
    row_of = block_codes // (pieces * KB)
    part_of = block_codes // KB % pieces
    inner_of = block_codes % KB
    selected = is_live & (part_of == part_index)
    row_hits = row_of[:, None] == jnp.arange(RB)[None, :]
    inner_hit = inner_of[:, None] == jnp.arange(KB)[None, :]
    weight = (selected[:, None, None] & row_hits[:, :, None] & inner_hit[:, None, :]).astype(
        jnp.bfloat16
    )
    dense_tile = jnp.einsum(
        "aik,axy->ixky", weight, block_stack, preferred_element_type=jnp.float32
    )
    return dense_tile.astype(jnp.bfloat16).reshape(RB * block_width, KB * block_width)


def dense_right(block_stack, block_codes):
    block_width = block_stack.shape[1]
    is_live = block_codes >= 0
    inner_of = block_codes // CB
    column_of = block_codes % CB
    inner_hit = inner_of[:, None] == jnp.arange(KB)[None, :]
    column_hit = column_of[:, None] == jnp.arange(CB)[None, :]
    weight = (is_live[:, None, None] & inner_hit[:, :, None] & column_hit[:, None, :]).astype(
        jnp.bfloat16
    )
    dense_tile = jnp.einsum(
        "skj,sxy->kxjy", weight, block_stack, preferred_element_type=jnp.float32
    )
    return dense_tile.astype(jnp.bfloat16).reshape(KB * block_width, CB * block_width)


def shards(a_blocks, a_codes, b_blocks, b_codes):
    row_count = lax.axis_size("row")
    col_count = lax.axis_size("col")
    pieces = row_count // col_count
    block_width = a_blocks.shape[1]
    row_index = lax.axis_index("row")
    col_index = lax.axis_index("col")
    a_stack, a_tags = (
        lax.all_to_all(a_blocks, "col", split_axis=0, concat_axis=0, tiled=True),
        lax.all_to_all(a_codes, "col", split_axis=0, concat_axis=0, tiled=True),
    )
    b_stack, b_tags = (
        lax.all_to_all(b_blocks, "row", split_axis=0, concat_axis=0, tiled=True),
        lax.all_to_all(b_codes, "row", split_axis=0, concat_axis=0, tiled=True),
    )

    def multiply(accumulated, left_stack, left_codes, right_stack, right_codes, piece_index):
        left_tile = dense_left(left_stack, left_codes, piece_index // col_count, pieces)
        right_tile = dense_right(right_stack, right_codes)
        return accumulated + jnp.dot(left_tile, right_tile, preferred_element_type=jnp.float32)

    start_sum = jnp.zeros((RB * block_width, CB * block_width), jnp.float32)

    def advance(visit_step, loop_state):
        accumulated, left_stack, left_codes, right_stack, right_codes = loop_state
        piece_index = (row_index + col_index + visit_step) % row_count
        accumulated = multiply(
            accumulated, left_stack, left_codes, right_stack, right_codes, piece_index
        )
        left_stack, left_codes = from_behind((left_stack, left_codes), "col", -1)
        right_stack, right_codes = from_behind((right_stack, right_codes), "row", -1)
        return (accumulated, left_stack, left_codes, right_stack, right_codes)

    loop_state = lax.fori_loop(
        0, row_count - 1, advance, (start_sum, a_stack, a_tags, b_stack, b_tags)
    )
    accumulated, left_stack, left_codes, right_stack, right_codes = loop_state
    last_piece = (row_index + col_index + row_count - 1) % row_count
    accumulated = multiply(
        accumulated, left_stack, left_codes, right_stack, right_codes, last_piece
    )
    reduced = lax.psum_scatter(accumulated, "layer", scatter_dimension=0, tiled=True)
    return reduced.astype(jnp.bfloat16)


WIDE = 16


def middle_plan(mesh_shape):
    return (mesh_shape["row"], mesh_shape["col"], mesh_shape["layer"]) == (4, 2, 4)


def pack_body(codes_ref, a_ref, b_ref, a_out, b_out):
    a_slots, width, _ = a_ref.shape
    b_slots = b_ref.shape[0]

    def code_rows(first, count):
        rows = lax.broadcasted_iota(jnp.int32, (WIDE, width), 0)
        values = jnp.full((WIDE, width), -1, jnp.int32)
        for slot in range(count):
            values = jnp.where(rows == slot, codes_ref[first + slot], values)
        return values.astype(jnp.float32).astype(jnp.bfloat16)

    for slot in range(a_slots):
        a_out[pl.ds(slot * width, width), :] = a_ref[slot]
    a_out[pl.ds(a_slots * width, WIDE), :] = code_rows(0, a_slots)
    for slot in range(b_slots):
        b_out[pl.ds(slot * width, width), :] = b_ref[slot]
    b_out[pl.ds(b_slots * width, WIDE), :] = code_rows(a_slots, b_slots)


def pack(codes, a_blocks, b_blocks):
    a_slots, width, _ = a_blocks.shape
    b_slots = b_blocks.shape[0]
    return pl.pallas_call(
        pack_body,
        out_shape=(
            jax.ShapeDtypeStruct((a_slots * width + WIDE, width), jnp.bfloat16),
            jax.ShapeDtypeStruct((b_slots * width + WIDE, width), jnp.bfloat16),
        ),
        in_specs=[
            pl.BlockSpec(memory_space=pltpu.SMEM),
            pl.BlockSpec(memory_space=pltpu.VMEM),
            pl.BlockSpec(memory_space=pltpu.VMEM),
        ],
        out_specs=(pl.BlockSpec(memory_space=pltpu.VMEM),) * 2,
        compiler_params=pltpu.CompilerParams(vmem_limit_bytes=16 << 20),
    )(codes, a_blocks, b_blocks)


def product_body(a_slots, b_slots, place_ref, a_codes, b_codes, *refs):
    a_refs, b_refs = refs[:4], refs[4:8]
    keep_ref, send_ref, dense, total = refs[8:]
    width = dense.shape[1] // CB
    pieces, owners_a, owners_b = 2, 2, 4
    is_middle, core, col, own_row, next_row = (place_ref[i] for i in range(5))
    rows_of_group = 2

    @pl.when(is_middle == 0)
    def _():
        keep_ref[...] = jnp.zeros_like(keep_ref)
        send_ref[...] = jnp.zeros_like(send_ref)

    @pl.when(is_middle == 1)
    def _():
        dense[...] = jnp.zeros_like(dense)
        total[...] = jnp.zeros_like(total)
        for source in range(4):
            for slot in range(b_slots):
                code = b_codes[source * b_slots + slot]

                @pl.when(code >= 0)
                def _():
                    piece = lax.rem(slot // (b_slots // owners_b) + col, owners_b)
                    inner = piece * KB + code // CB
                    column = lax.rem(code, CB)
                    dense[
                        pl.ds(pl.multiple_of(inner * width, width), width),
                        pl.ds(pl.multiple_of(column * width, width), width),
                    ] = b_refs[source][pl.ds(slot * width, width), :]

        for group in range(2):
            row = (own_row, next_row)[group]
            for source in (2 * group, 2 * group + 1):
                for slot in range(a_slots):
                    code = a_codes[source * a_slots + slot]
                    live = (code >= 0).astype(jnp.int32)
                    safe = jnp.maximum(code, 0)
                    owner = slot // (a_slots // owners_a)
                    piece = lax.rem(row + owner, owners_a) + owners_a * lax.rem(safe // KB, pieces)
                    inner = piece * KB + lax.rem(safe, KB)
                    block_row = safe // (pieces * KB)
                    sent = lax.rem(block_row, rows_of_group) != core
                    spot = sent.astype(jnp.int32) * 4 + group * 2 + block_row // rows_of_group
                    spot = live * spot + (1 - live) * 8
                    part = jnp.dot(
                        a_refs[source][pl.ds(slot * width, width), :],
                        dense[pl.ds(pl.multiple_of(inner * width, width), width), :],
                        preferred_element_type=jnp.float32,
                    )
                    total[pl.ds(pl.multiple_of(spot * width, width), width), :] += part
        keep_ref[...] = total[pl.ds(0, 4 * width), :]
        send_ref[...] = total[pl.ds(4 * width, 4 * width), :]


def product(place, a_codes, b_codes, a_packs, b_packs, a_slots, b_slots):
    width = a_packs[0].shape[1]
    smem, vmem = pl.BlockSpec(memory_space=pltpu.SMEM), pl.BlockSpec(memory_space=pltpu.VMEM)
    half = jax.ShapeDtypeStruct((4 * width, CB * width), jnp.float32)
    return pl.pallas_call(
        functools.partial(product_body, a_slots, b_slots),
        out_shape=(half, half),
        in_specs=[smem] * 3 + [vmem] * 8,
        out_specs=(vmem, vmem),
        scratch_shapes=[
            pltpu.VMEM((4 * KB * width, CB * width), jnp.bfloat16),
            pltpu.VMEM((9 * width, CB * width), jnp.float32),
        ],
        compiler_params=pltpu.CompilerParams(vmem_limit_bytes=32 << 20),
        cost_estimate=pl.CostEstimate(flops=6 << 30, bytes_accessed=8 << 20, transcendentals=0),
    )(place, a_codes, b_codes, *a_packs, *b_packs)


TO_MIDDLE = [(0, 1), (3, 2)]
MIDDLE = [(1, 2), (2, 1)]


def middle_shards(a_blocks, a_codes, b_blocks, b_codes):
    a_slots, width, _ = a_blocks.shape
    b_slots = b_blocks.shape[0]
    row, col, layer = (lax.axis_index(name) for name in ("row", "col", "layer"))
    chip, core = layer // 2, layer % 2
    is_middle = ((row == 1) | (row == 2)).astype(jnp.int32)
    next_row = jnp.where(row == 1, 0, 3)
    place = jnp.stack([is_middle, core, col, row, next_row]).astype(jnp.int32)

    a_pack, b_pack = pack(jnp.concatenate([a_codes, b_codes]), a_blocks, b_blocks)
    b_across = lax.ppermute(b_pack, "row", MIDDLE)
    b_end = lax.ppermute(b_pack, "row", TO_MIDDLE)
    a_other = lax.ppermute(a_pack, "col", [(0, 1), (1, 0)])
    a_end = lax.ppermute(a_pack, "row", TO_MIDDLE)
    b_far = lax.ppermute(b_end, "row", MIDDLE)
    rows_cols = [(r * 2 + c, r * 2 + 1 - c) for r in (1, 2) for c in (0, 1)]
    a_end_other = lax.ppermute(a_end, ("row", "col"), rows_cols)

    a_packs = (a_pack, a_other, a_end, a_end_other)
    b_packs = (b_pack, b_across, b_end, b_far)

    def codes_of(packs, slots):
        first = slots * width
        tails = [lax.slice(p, (first, 0), (first + slots, 1)) for p in packs]
        return jnp.concatenate(tails)[:, 0].astype(jnp.int32)

    keep, send = product(
        place, codes_of(a_packs, a_slots), codes_of(b_packs, b_slots), a_packs, b_packs, a_slots, b_slots
    )
    cores = [(r * 4 + m, r * 4 + (m ^ 1)) for r in (1, 2) for m in range(4)]
    summed = keep + lax.ppermute(send, ("row", "layer"), cores)
    summed = summed.reshape(2, 2, width, CB * width)
    near = lax.dynamic_index_in_dim(summed, chip, axis=1, keepdims=False)
    far = lax.dynamic_index_in_dim(summed, 1 - chip, axis=1, keepdims=False)
    ends = ((1, 0), (2, 3))
    across = [(s * 4 + m, e * 4 + (m ^ 2)) for s, e in ends for m in range(4)]
    along = [(s * 4 + m, e * 4 + m) for s, e in ends for m in range(4)]
    chips = [(r * 4 + m, r * 4 + (m ^ 2)) for r in (1, 2) for m in range(4)]
    out = near[0]
    out = out + lax.ppermute(far[1], ("row", "layer"), across)
    out = out + lax.ppermute(far[0], ("row", "layer"), chips)
    out = out + lax.ppermute(near[1], ("row", "layer"), along)
    return out.astype(jnp.bfloat16)


def solution(mesh):
    placed = (
        P(("row", "col", "layer"), None, None),
        P(("row", "col", "layer")),
        P(("row", "col", "layer"), None, None),
        P(("row", "col", "layer")),
    )
    body = middle_shards if middle_plan(mesh.shape) else shards
    return jax.shard_map(
        body, mesh=mesh, in_specs=placed, out_specs=P(("row", "layer"), "col"), check_vma=False
    )
```

```python
import functools

import jax
import jax.numpy as jnp
from jax import lax
from jax.experimental import pallas as pl
from jax.experimental.pallas import tpu as pltpu
from jax.sharding import PartitionSpec as P

RB = 4
CB = 4
KB = 6


def from_behind(block, axis, distance):
    devices = range(lax.axis_size(axis))
    route = [((i - distance) % len(devices), i) for i in devices]
    return lax.ppermute(block, axis, route)


def dense_left(block_stack, block_codes, part_index, pieces):
    block_width = block_stack.shape[1]
    is_live = block_codes >= 0
    row_of = block_codes // (pieces * KB)
    part_of = block_codes // KB % pieces
    inner_of = block_codes % KB
    selected = is_live & (part_of == part_index)
    row_hits = row_of[:, None] == jnp.arange(RB)[None, :]
    inner_hit = inner_of[:, None] == jnp.arange(KB)[None, :]
    weight = (selected[:, None, None] & row_hits[:, :, None] & inner_hit[:, None, :]).astype(
        jnp.bfloat16
    )
    dense_tile = jnp.einsum(
        "aik,axy->ixky", weight, block_stack, preferred_element_type=jnp.float32
    )
    return dense_tile.astype(jnp.bfloat16).reshape(RB * block_width, KB * block_width)


def dense_right(block_stack, block_codes):
    block_width = block_stack.shape[1]
    is_live = block_codes >= 0
    inner_of = block_codes // CB
    column_of = block_codes % CB
    inner_hit = inner_of[:, None] == jnp.arange(KB)[None, :]
    column_hit = column_of[:, None] == jnp.arange(CB)[None, :]
    weight = (is_live[:, None, None] & inner_hit[:, :, None] & column_hit[:, None, :]).astype(
        jnp.bfloat16
    )
    dense_tile = jnp.einsum(
        "skj,sxy->kxjy", weight, block_stack, preferred_element_type=jnp.float32
    )
    return dense_tile.astype(jnp.bfloat16).reshape(KB * block_width, CB * block_width)


def shards(a_blocks, a_codes, b_blocks, b_codes):
    row_count = lax.axis_size("row")
    col_count = lax.axis_size("col")
    pieces = row_count // col_count
    block_width = a_blocks.shape[1]
    row_index = lax.axis_index("row")
    col_index = lax.axis_index("col")
    a_stack, a_tags = (
        lax.all_to_all(a_blocks, "col", split_axis=0, concat_axis=0, tiled=True),
        lax.all_to_all(a_codes, "col", split_axis=0, concat_axis=0, tiled=True),
    )
    b_stack, b_tags = (
        lax.all_to_all(b_blocks, "row", split_axis=0, concat_axis=0, tiled=True),
        lax.all_to_all(b_codes, "row", split_axis=0, concat_axis=0, tiled=True),
    )

    def multiply(accumulated, left_stack, left_codes, right_stack, right_codes, piece_index):
        left_tile = dense_left(left_stack, left_codes, piece_index // col_count, pieces)
        right_tile = dense_right(right_stack, right_codes)
        return accumulated + jnp.dot(left_tile, right_tile, preferred_element_type=jnp.float32)

    start_sum = jnp.zeros((RB * block_width, CB * block_width), jnp.float32)

    def advance(visit_step, loop_state):
        accumulated, left_stack, left_codes, right_stack, right_codes = loop_state
        piece_index = (row_index + col_index + visit_step) % row_count
        accumulated = multiply(
            accumulated, left_stack, left_codes, right_stack, right_codes, piece_index
        )
        left_stack, left_codes = from_behind((left_stack, left_codes), "col", -1)
        right_stack, right_codes = from_behind((right_stack, right_codes), "row", -1)
        return (accumulated, left_stack, left_codes, right_stack, right_codes)

    loop_state = lax.fori_loop(
        0, row_count - 1, advance, (start_sum, a_stack, a_tags, b_stack, b_tags)
    )
    accumulated, left_stack, left_codes, right_stack, right_codes = loop_state
    last_piece = (row_index + col_index + row_count - 1) % row_count
    accumulated = multiply(
        accumulated, left_stack, left_codes, right_stack, right_codes, last_piece
    )
    reduced = lax.psum_scatter(accumulated, "layer", scatter_dimension=0, tiled=True)
    return reduced.astype(jnp.bfloat16)


CODE_ROWS = 16


def middle_plan(mesh_shape):
    return (mesh_shape["row"], mesh_shape["col"], mesh_shape["layer"]) == (4, 2, 4)


def spaces(*names):
    kinds = {"s": pltpu.SMEM, "v": pltpu.VMEM, "h": pltpu.HBM}
    return [pl.BlockSpec(memory_space=kinds[name]) for name in names]


def pack_body(a_codes, b_codes, a_ref, b_ref, a_out, b_out, first_out, second_out, sems):
    a_rows, b_rows = a_ref.shape[0], b_ref.shape[0]
    width = a_ref.shape[1]
    half = b_rows // 2
    copies = [
        pltpu.make_async_copy(b_ref.at[pl.ds(0, half)], first_out.at[pl.ds(0, half)], sems.at[0]),
        pltpu.make_async_copy(b_ref, b_out.at[pl.ds(0, b_rows)], sems.at[1]),
        pltpu.make_async_copy(b_ref.at[pl.ds(half, half)], second_out, sems.at[2]),
        pltpu.make_async_copy(a_ref, a_out.at[pl.ds(0, a_rows)], sems.at[3]),
    ]
    for copy in copies:
        copy.start()

    def code_rows(codes_ref):
        lanes = lax.broadcasted_iota(jnp.int32, (CODE_ROWS, width), 1)
        values = jnp.full((CODE_ROWS, width), -1, jnp.int32)
        for slot in range(codes_ref.shape[0]):
            values = jnp.where(lanes == slot, codes_ref[slot], values)
        return values.astype(jnp.float32).astype(jnp.bfloat16)

    a_out[pl.ds(a_rows, CODE_ROWS), :] = code_rows(a_codes)
    b_tail = code_rows(b_codes)
    b_out[pl.ds(b_rows, CODE_ROWS), :] = b_tail
    first_out[pl.ds(half, CODE_ROWS), :] = b_tail
    for copy in copies:
        copy.wait()


def pack(a_codes, b_codes, a_blocks, b_blocks):
    width = a_blocks.shape[1]
    a_flat = a_blocks.reshape(-1, width)
    b_flat = b_blocks.reshape(-1, width)
    a_rows, b_rows = a_flat.shape[0], b_flat.shape[0]
    sizes = (a_rows + CODE_ROWS, b_rows + CODE_ROWS, b_rows // 2 + CODE_ROWS, b_rows // 2)
    return pl.pallas_call(
        pack_body,
        out_shape=tuple(jax.ShapeDtypeStruct((rows, width), jnp.bfloat16) for rows in sizes),
        in_specs=spaces("s", "s", "h", "h"),
        out_specs=tuple(spaces("v", "v", "v", "v")),
        scratch_shapes=[pltpu.SemaphoreType.DMA((4,))],
        compiler_params=pltpu.CompilerParams(vmem_limit_bytes=8 << 20),
    )(*(pltpu.with_memory_space_constraint(x, pltpu.HBM) for x in (a_codes, b_codes, a_flat, b_flat)))


def fetch_codes(packs, staged, codes, sem):
    for index, pack_ref in enumerate(packs):
        tail = pack_ref[pl.ds(pack_ref.shape[0] - CODE_ROWS, CODE_ROWS), :]
        staged[pl.ds(index, 1), :] = tail.astype(jnp.float32).astype(jnp.int32)[:1]
    return pltpu.make_async_copy(staged, codes, sem)


def code_scratch():
    return [
        pltpu.VMEM((8, 128), jnp.int32),
        pltpu.SMEM((8, 128), jnp.int32),
        pltpu.SemaphoreType.DMA(()),
    ]


def in_middle():
    row = lax.axis_index("row")
    return jnp.logical_or(row == 1, row == 2)


def put_blocks(dense, source, codes, line, first_slot, count, slots, col):
    width = source.shape[1]
    owners = 4
    for index in range(count):
        code = codes[line, first_slot + index]

        @pl.when(code >= 0)
        def _():
            piece = lax.rem((first_slot + index) // (slots // owners) + col, owners)
            inner = piece * KB + code // CB
            column = lax.rem(code, CB)
            dense[
                pl.ds(pl.multiple_of(inner * width, width), width),
                pl.ds(pl.multiple_of(column * width, width), width),
            ] = source[pl.ds(index * width, width), :]


def early_body(slots, own, across, first, second, far, other, dense, staged, codes, sem):
    del other
    half = slots // 2

    @pl.when(in_middle())
    def _():
        col = lax.axis_index("col")
        copy = fetch_codes((own, across, first, far), staged, codes, sem)
        copy.start()
        dense[...] = jnp.zeros_like(dense)
        copy.wait()
        put_blocks(dense, own, codes, 0, 0, slots, slots, col)
        put_blocks(dense, across, codes, 1, 0, slots, slots, col)
        put_blocks(dense, first, codes, 2, 0, half, slots, col)
        put_blocks(dense, second, codes, 2, half, half, slots, col)
        put_blocks(dense, far, codes, 3, 0, half, slots, col)


def early(own, across, first, second, far, other, slots):
    width = own.shape[1]
    return pl.pallas_call(
        functools.partial(early_body, slots),
        out_shape=jax.ShapeDtypeStruct((4 * KB * width, CB * width), jnp.bfloat16),
        in_specs=spaces("v", "v", "v", "v", "v", "h"),
        out_specs=spaces("v")[0],
        scratch_shapes=code_scratch(),
        compiler_params=pltpu.CompilerParams(vmem_limit_bytes=12 << 20),
    )(own, across, first, second, far, other)


def multiply_group(dense, total, packs, codes, slots, row):
    width = packs[0].shape[1]
    pieces, owners = 2, 2
    core = lax.rem(lax.axis_index("layer"), 2)
    total[...] = jnp.zeros_like(total)
    for source in range(2):
        for slot in range(slots):
            code = codes[source, slot]
            live = (code >= 0).astype(jnp.int32)
            safe = jnp.maximum(code, 0)
            owner = slot // (slots // owners)
            piece = lax.rem(row + owner, owners) + owners * lax.rem(safe // KB, pieces)
            inner = piece * KB + lax.rem(safe, KB)
            block_row = safe // (pieces * KB)
            sent = (lax.rem(block_row, 2) != core).astype(jnp.int32)
            spot = live * (sent * 2 + block_row // 2) + (1 - live) * 4
            part = jnp.dot(
                packs[source][pl.ds(slot * width, width), :],
                dense[pl.ds(pl.multiple_of(inner * width, width), width), :],
                preferred_element_type=jnp.float32,
            )
            total[pl.ds(pl.multiple_of(spot * width, width), width), :] += part


def end_body(a_slots, slots, packs_0, packs_1, dense_in, first, second,
             dense, keep, send, total, staged, codes, sem):
    half = slots // 2
    rows = keep.shape[0]
    del dense_in

    @pl.when(in_middle())
    def _():
        copy = fetch_codes((packs_0, packs_1, first), staged, codes, sem)
        copy.start()
        copy.wait()
        put_blocks(dense, second, codes, 2, half, half, slots, lax.axis_index("col"))
        row = jnp.where(lax.axis_index("row") == 1, 0, 3)
        multiply_group(dense, total, (packs_0, packs_1), codes, a_slots, row)
        keep[...] = total[pl.ds(0, rows), :]
        send[...] = total[pl.ds(rows, rows), :]


def own_body(a_slots, packs_0, packs_1, dense, keep, send, total, staged, codes, sem):
    rows = keep.shape[0]

    @pl.when(jnp.logical_not(in_middle()))
    def _():
        keep[...] = jnp.zeros_like(keep)

    @pl.when(in_middle())
    def _():
        copy = fetch_codes((packs_0, packs_1), staged, codes, sem)
        copy.start()
        copy.wait()
        multiply_group(dense, total, (packs_0, packs_1), codes, a_slots, lax.axis_index("row"))
        keep[...] = total[pl.ds(0, rows), :]
        send[...] = total[pl.ds(rows, rows), :]


def end_product(packs, dense, first, second, a_slots, slots):
    width = packs[0].shape[1]
    half = jax.ShapeDtypeStruct((2 * width, CB * width), jnp.float32)
    return pl.pallas_call(
        functools.partial(end_body, a_slots, slots),
        out_shape=(jax.ShapeDtypeStruct(dense.shape, dense.dtype), half, half),
        in_specs=spaces("v", "v", "v", "v", "v"),
        out_specs=tuple(spaces("v", "v", "v")),
        scratch_shapes=[pltpu.VMEM((5 * width, CB * width), jnp.float32)] + code_scratch(),
        input_output_aliases={2: 0},
        compiler_params=pltpu.CompilerParams(vmem_limit_bytes=16 << 20),
    )(*packs, dense, first, second)


def own_product(packs, dense, a_slots):
    width = packs[0].shape[1]
    half = jax.ShapeDtypeStruct((2 * width, CB * width), jnp.float32)
    return pl.pallas_call(
        functools.partial(own_body, a_slots),
        out_shape=(half, half),
        in_specs=spaces("v", "v", "v"),
        out_specs=tuple(spaces("v", "v")),
        scratch_shapes=[pltpu.VMEM((5 * width, CB * width), jnp.float32)] + code_scratch(),
        compiler_params=pltpu.CompilerParams(vmem_limit_bytes=16 << 20),
    )(*packs, dense)


def fold_body(keep, got, near, far):
    rows = near.shape[0]
    chip = lax.axis_index("layer") // 2
    for out, index in ((near, chip), (far, 1 - chip)):
        block = pl.ds(pl.multiple_of(index * rows, rows), rows)
        out[...] = keep[block, :] + got[block, :]


def fold(keep, got):
    rows, width = keep.shape
    half = jax.ShapeDtypeStruct((rows // 2, width), keep.dtype)
    return pl.pallas_call(
        fold_body,
        out_shape=(half, half),
        in_specs=spaces("v", "v"),
        out_specs=tuple(spaces("v", "v")),
        compiler_params=pltpu.CompilerParams(vmem_limit_bytes=4 << 20),
    )(keep, got)


BESIDE = [(0, 1), (3, 2)]
BEYOND = [(0, 2), (3, 1)]
MIDDLE = [(1, 2), (2, 1)]


def middle_shards(a_blocks, a_codes, b_blocks, b_codes):
    a_slots, slots = a_blocks.shape[0], b_blocks.shape[0]
    a_pack, b_pack, b_first, b_second = pack(a_codes, b_codes, a_blocks, b_blocks)
    b_across = lax.ppermute(b_pack, "row", MIDDLE)
    end_first = lax.ppermute(b_first, "row", BESIDE)
    a_other = lax.ppermute(a_pack, "col", [(0, 1), (1, 0)])
    a_end = lax.ppermute(a_pack, "row", BESIDE)
    end_second = lax.ppermute(b_second, "row", BESIDE)
    far_first = lax.ppermute(end_first, "row", MIDDLE)
    far_second = lax.ppermute(end_second, "row", MIDDLE)
    rows_cols = [(r * 2 + c, r * 2 + 1 - c) for r in (1, 2) for c in (0, 1)]
    a_end_other = lax.ppermute(a_end, ("row", "col"), rows_cols)

    dense = early(b_pack, b_across, end_first, end_second, far_first, a_other, slots)
    dense, end_keep, end_send = end_product(
        (a_end, a_end_other), dense, far_first, far_second, a_slots, slots
    )
    own_keep, own_send = own_product((a_pack, a_other), dense, a_slots)

    cores = [(r * 4 + m, r * 4 + (m ^ 1)) for r in (1, 2) for m in range(4)]
    ends = ((1, 0), (2, 3))
    across = [(s * 4 + m, e * 4 + (m ^ 2)) for s, e in ends for m in range(4)]
    along = [(s * 4 + m, e * 4 + m) for s, e in ends for m in range(4)]
    chips = [(r * 4 + m, r * 4 + (m ^ 2)) for r in (1, 2) for m in range(4)]

    def over_cores(keep, send):
        return fold(keep, lax.ppermute(send, ("row", "layer"), cores))

    near, far = over_cores(end_keep, end_send)
    out = lax.ppermute(near, ("row", "layer"), along)
    out = out + lax.ppermute(far, ("row", "layer"), across)
    own_send, _ = lax.optimization_barrier((own_send, near))
    near, far = over_cores(own_keep, own_send)
    out = out + near
    out = out + lax.ppermute(far, ("row", "layer"), chips)
    return out.astype(jnp.bfloat16)


def solution(mesh):
    placed = (
        P(("row", "col", "layer"), None, None),
        P(("row", "col", "layer")),
        P(("row", "col", "layer"), None, None),
        P(("row", "col", "layer")),
    )
    body = middle_shards if middle_plan(mesh.shape) else shards
    return jax.shard_map(
        body, mesh=mesh, in_specs=placed, out_specs=P(("row", "layer"), "col"), check_vma=False
    )
```

```python
import functools

import jax
import jax.numpy as jnp
from jax import lax
from jax.experimental import pallas as pl
from jax.experimental.pallas import tpu as pltpu
from jax.sharding import PartitionSpec as P

RB = 4
CB = 4
KB = 6


def from_behind(block, axis, distance):
    devices = range(lax.axis_size(axis))
    route = [((i - distance) % len(devices), i) for i in devices]
    return lax.ppermute(block, axis, route)


def dense_left(block_stack, block_codes, part_index, pieces):
    block_width = block_stack.shape[1]
    is_live = block_codes >= 0
    row_of = block_codes // (pieces * KB)
    part_of = block_codes // KB % pieces
    inner_of = block_codes % KB
    selected = is_live & (part_of == part_index)
    row_hits = row_of[:, None] == jnp.arange(RB)[None, :]
    inner_hit = inner_of[:, None] == jnp.arange(KB)[None, :]
    weight = (selected[:, None, None] & row_hits[:, :, None] & inner_hit[:, None, :]).astype(
        jnp.bfloat16
    )
    dense_tile = jnp.einsum(
        "aik,axy->ixky", weight, block_stack, preferred_element_type=jnp.float32
    )
    return dense_tile.astype(jnp.bfloat16).reshape(RB * block_width, KB * block_width)


def dense_right(block_stack, block_codes):
    block_width = block_stack.shape[1]
    is_live = block_codes >= 0
    inner_of = block_codes // CB
    column_of = block_codes % CB
    inner_hit = inner_of[:, None] == jnp.arange(KB)[None, :]
    column_hit = column_of[:, None] == jnp.arange(CB)[None, :]
    weight = (is_live[:, None, None] & inner_hit[:, :, None] & column_hit[:, None, :]).astype(
        jnp.bfloat16
    )
    dense_tile = jnp.einsum(
        "skj,sxy->kxjy", weight, block_stack, preferred_element_type=jnp.float32
    )
    return dense_tile.astype(jnp.bfloat16).reshape(KB * block_width, CB * block_width)


def shards(a_blocks, a_codes, b_blocks, b_codes):
    row_count = lax.axis_size("row")
    col_count = lax.axis_size("col")
    pieces = row_count // col_count
    block_width = a_blocks.shape[1]
    row_index = lax.axis_index("row")
    col_index = lax.axis_index("col")
    a_stack, a_tags = (
        lax.all_to_all(a_blocks, "col", split_axis=0, concat_axis=0, tiled=True),
        lax.all_to_all(a_codes, "col", split_axis=0, concat_axis=0, tiled=True),
    )
    b_stack, b_tags = (
        lax.all_to_all(b_blocks, "row", split_axis=0, concat_axis=0, tiled=True),
        lax.all_to_all(b_codes, "row", split_axis=0, concat_axis=0, tiled=True),
    )

    def multiply(accumulated, left_stack, left_codes, right_stack, right_codes, piece_index):
        left_tile = dense_left(left_stack, left_codes, piece_index // col_count, pieces)
        right_tile = dense_right(right_stack, right_codes)
        return accumulated + jnp.dot(left_tile, right_tile, preferred_element_type=jnp.float32)

    start_sum = jnp.zeros((RB * block_width, CB * block_width), jnp.float32)

    def advance(visit_step, loop_state):
        accumulated, left_stack, left_codes, right_stack, right_codes = loop_state
        piece_index = (row_index + col_index + visit_step) % row_count
        accumulated = multiply(
            accumulated, left_stack, left_codes, right_stack, right_codes, piece_index
        )
        left_stack, left_codes = from_behind((left_stack, left_codes), "col", -1)
        right_stack, right_codes = from_behind((right_stack, right_codes), "row", -1)
        return (accumulated, left_stack, left_codes, right_stack, right_codes)

    loop_state = lax.fori_loop(
        0, row_count - 1, advance, (start_sum, a_stack, a_tags, b_stack, b_tags)
    )
    accumulated, left_stack, left_codes, right_stack, right_codes = loop_state
    last_piece = (row_index + col_index + row_count - 1) % row_count
    accumulated = multiply(
        accumulated, left_stack, left_codes, right_stack, right_codes, last_piece
    )
    reduced = lax.psum_scatter(accumulated, "layer", scatter_dimension=0, tiled=True)
    return reduced.astype(jnp.bfloat16)


CODE_ROWS = 16
FIRST = 8


def middle_plan(mesh_shape):
    return (mesh_shape["row"], mesh_shape["col"], mesh_shape["layer"]) == (4, 2, 4)


def spaces(*names):
    kinds = {"s": pltpu.SMEM, "v": pltpu.VMEM, "h": pltpu.HBM}
    return [pl.BlockSpec(memory_space=kinds[name]) for name in names]


def first_slots(slots):
    return slots * FIRST // 16


def pack_body(a_codes, b_codes, a_ref, b_ref, a_out, b_out, mixed_out, second_out, sems):
    a_rows, b_rows = a_ref.shape[0], b_ref.shape[0]
    width = a_ref.shape[1]
    second = second_out.shape[0] - CODE_ROWS
    first = b_rows - second
    copies = [
        pltpu.make_async_copy(b_ref, b_out.at[pl.ds(0, b_rows)], sems.at[0]),
        pltpu.make_async_copy(b_ref.at[pl.ds(0, first)], mixed_out.at[pl.ds(0, first)], sems.at[1]),
        pltpu.make_async_copy(a_ref, mixed_out.at[pl.ds(first + CODE_ROWS, a_rows)], sems.at[2]),
        pltpu.make_async_copy(b_ref.at[pl.ds(first, second)], second_out.at[pl.ds(0, second)], sems.at[3]),
        pltpu.make_async_copy(a_ref, a_out.at[pl.ds(0, a_rows)], sems.at[4]),
    ]
    for copy in copies:
        copy.start()

    def code_rows(codes_ref):
        lanes = lax.broadcasted_iota(jnp.int32, (CODE_ROWS, width), 1)
        values = jnp.full((CODE_ROWS, width), -1, jnp.int32)
        for slot in range(codes_ref.shape[0]):
            values = jnp.where(lanes == slot, codes_ref[slot], values)
        return values.astype(jnp.float32).astype(jnp.bfloat16)

    a_tail, b_tail = code_rows(a_codes), code_rows(b_codes)
    a_out[pl.ds(a_rows, CODE_ROWS), :] = a_tail
    b_out[pl.ds(b_rows, CODE_ROWS), :] = b_tail
    mixed_out[pl.ds(first, CODE_ROWS), :] = b_tail
    mixed_out[pl.ds(first + CODE_ROWS + a_rows, CODE_ROWS), :] = a_tail
    second_out[pl.ds(second, CODE_ROWS), :] = b_tail
    for copy in copies:
        copy.wait()


def pack(a_codes, b_codes, a_blocks, b_blocks):
    width = a_blocks.shape[1]
    a_flat = a_blocks.reshape(-1, width)
    b_flat = b_blocks.reshape(-1, width)
    a_rows, b_rows = a_flat.shape[0], b_flat.shape[0]
    first = first_slots(b_blocks.shape[0]) * width
    sizes = (
        a_rows + CODE_ROWS,
        b_rows + CODE_ROWS,
        first + a_rows + 2 * CODE_ROWS,
        b_rows - first + CODE_ROWS,
    )
    return pl.pallas_call(
        pack_body,
        out_shape=tuple(jax.ShapeDtypeStruct((rows, width), jnp.bfloat16) for rows in sizes),
        in_specs=spaces("s", "s", "h", "h"),
        out_specs=tuple(spaces("v", "v", "v", "v")),
        scratch_shapes=[pltpu.SemaphoreType.DMA((5,))],
        compiler_params=pltpu.CompilerParams(vmem_limit_bytes=8 << 20),
    )(*(pltpu.with_memory_space_constraint(x, pltpu.HBM) for x in (a_codes, b_codes, a_flat, b_flat)))


def part_body(mixed, first, second):
    rows = first.shape[0]
    first[...] = mixed[pl.ds(0, rows), :]
    second[...] = mixed[pl.ds(rows, second.shape[0]), :]


def part(mixed, rows):
    sizes = (rows, mixed.shape[0] - rows)
    return pl.pallas_call(
        part_body,
        out_shape=tuple(jax.ShapeDtypeStruct((n, mixed.shape[1]), mixed.dtype) for n in sizes),
        in_specs=spaces("v"),
        out_specs=tuple(spaces("v", "v")),
        compiler_params=pltpu.CompilerParams(vmem_limit_bytes=4 << 20),
    )(mixed)


def fetch_codes(packs, staged, codes, sem):
    for index, pack_ref in enumerate(packs):
        tail = pack_ref[pl.ds(pack_ref.shape[0] - CODE_ROWS, CODE_ROWS), :]
        staged[pl.ds(index, 1), :] = tail.astype(jnp.float32).astype(jnp.int32)[:1]
    return pltpu.make_async_copy(staged, codes, sem)


def code_scratch():
    return [
        pltpu.VMEM((8, 128), jnp.int32),
        pltpu.SMEM((8, 128), jnp.int32),
        pltpu.SemaphoreType.DMA(()),
    ]


def in_middle():
    row = lax.axis_index("row")
    return jnp.logical_or(row == 1, row == 2)


def put_blocks(dense, source, codes, line, first_slot, count, slots, col):
    width = source.shape[1]
    owners = 4
    for index in range(count):
        code = codes[line, first_slot + index]

        @pl.when(code >= 0)
        def _():
            piece = lax.rem((first_slot + index) // (slots // owners) + col, owners)
            inner = piece * KB + code // CB
            column = lax.rem(code, CB)
            dense[
                pl.ds(pl.multiple_of(inner * width, width), width),
                pl.ds(pl.multiple_of(column * width, width), width),
            ] = source[pl.ds(index * width, width), :]


def early_body(slots, own, across, first, second, far, other, dense, staged, codes, sem):
    del other
    cut = first_slots(slots)

    @pl.when(in_middle())
    def _():
        col = lax.axis_index("col")
        copy = fetch_codes((own, across, first, far), staged, codes, sem)
        copy.start()
        dense[...] = jnp.zeros_like(dense)
        copy.wait()
        put_blocks(dense, own, codes, 0, 0, slots, slots, col)
        put_blocks(dense, across, codes, 1, 0, slots, slots, col)
        put_blocks(dense, first, codes, 2, 0, cut, slots, col)
        put_blocks(dense, second, codes, 2, cut, slots - cut, slots, col)
        put_blocks(dense, far, codes, 3, cut, slots - cut, slots, col)


def early(own, across, first, second, far, other, slots):
    width = own.shape[1]
    return pl.pallas_call(
        functools.partial(early_body, slots),
        out_shape=jax.ShapeDtypeStruct((4 * KB * width, CB * width), jnp.bfloat16),
        in_specs=spaces("v", "v", "v", "v", "v", "h"),
        out_specs=spaces("v")[0],
        scratch_shapes=code_scratch(),
        compiler_params=pltpu.CompilerParams(vmem_limit_bytes=12 << 20),
    )(own, across, first, second, far, other)


def multiply_group(dense, total, packs, codes, slots, row):
    width = packs[0].shape[1]
    pieces, owners = 2, 2
    core = lax.rem(lax.axis_index("layer"), 2)
    total[...] = jnp.zeros_like(total)
    for source in range(2):
        for slot in range(slots):
            code = codes[source, slot]
            live = (code >= 0).astype(jnp.int32)
            safe = jnp.maximum(code, 0)
            owner = slot // (slots // owners)
            piece = lax.rem(row + owner, owners) + owners * lax.rem(safe // KB, pieces)
            inner = piece * KB + lax.rem(safe, KB)
            block_row = safe // (pieces * KB)
            sent = (lax.rem(block_row, 2) != core).astype(jnp.int32)
            spot = live * (sent * 2 + block_row // 2) + (1 - live) * 4
            part = jnp.dot(
                packs[source][pl.ds(slot * width, width), :],
                dense[pl.ds(pl.multiple_of(inner * width, width), width), :],
                preferred_element_type=jnp.float32,
            )
            total[pl.ds(pl.multiple_of(spot * width, width), width), :] += part


def own_body(a_slots, slots, packs_0, packs_1, dense_in, first,
             dense, keep, send, total, staged, codes, sem):
    cut = first_slots(slots)
    rows = keep.shape[0]
    del dense_in

    @pl.when(jnp.logical_not(in_middle()))
    def _():
        keep[...] = jnp.zeros_like(keep)
        send[...] = jnp.zeros_like(send)

    @pl.when(in_middle())
    def _():
        copy = fetch_codes((packs_0, packs_1, first), staged, codes, sem)
        copy.start()
        copy.wait()
        col = lax.axis_index("col")
        put_blocks(dense, first, codes, 2, 0, cut, slots, col)
        multiply_group(dense, total, (packs_0, packs_1), codes, a_slots, lax.axis_index("row"))
        keep[...] = total[pl.ds(0, rows), :]
        send[...] = total[pl.ds(rows, rows), :]


def end_body(a_slots, packs_0, packs_1, dense, keep, send, total, staged, codes, sem):
    rows = keep.shape[0]

    @pl.when(jnp.logical_not(in_middle()))
    def _():
        keep[...] = jnp.zeros_like(keep)
        send[...] = jnp.zeros_like(send)

    @pl.when(in_middle())
    def _():
        copy = fetch_codes((packs_0, packs_1), staged, codes, sem)
        copy.start()
        copy.wait()
        row = jnp.where(lax.axis_index("row") == 1, 0, 3)
        multiply_group(dense, total, (packs_0, packs_1), codes, a_slots, row)
        keep[...] = total[pl.ds(0, rows), :]
        send[...] = total[pl.ds(rows, rows), :]


def own_product(packs, dense, first, a_slots, slots):
    width = packs[0].shape[1]
    half = jax.ShapeDtypeStruct((2 * width, CB * width), jnp.float32)
    return pl.pallas_call(
        functools.partial(own_body, a_slots, slots),
        out_shape=(jax.ShapeDtypeStruct(dense.shape, dense.dtype), half, half),
        in_specs=spaces("v", "v", "v", "v"),
        out_specs=tuple(spaces("v", "v", "v")),
        scratch_shapes=[pltpu.VMEM((5 * width, CB * width), jnp.float32)] + code_scratch(),
        input_output_aliases={2: 0},
        compiler_params=pltpu.CompilerParams(vmem_limit_bytes=16 << 20),
    )(*packs, dense, first)


def end_product(packs, dense, a_slots):
    width = packs[0].shape[1]
    half = jax.ShapeDtypeStruct((2 * width, CB * width), jnp.float32)
    return pl.pallas_call(
        functools.partial(end_body, a_slots),
        out_shape=(half, half),
        in_specs=spaces("v", "v", "v"),
        out_specs=tuple(spaces("v", "v")),
        scratch_shapes=[pltpu.VMEM((5 * width, CB * width), jnp.float32)] + code_scratch(),
        compiler_params=pltpu.CompilerParams(vmem_limit_bytes=16 << 20),
    )(*packs, dense)


def fold_body(keep, got, near, far):
    rows = near.shape[0]
    chip = lax.axis_index("layer") // 2
    for out, index in ((near, chip), (far, 1 - chip)):
        block = pl.ds(pl.multiple_of(index * rows, rows), rows)
        out[...] = keep[block, :] + got[block, :]


def fold(keep, got):
    rows, width = keep.shape
    half = jax.ShapeDtypeStruct((rows // 2, width), keep.dtype)
    return pl.pallas_call(
        fold_body,
        out_shape=(half, half),
        in_specs=spaces("v", "v"),
        out_specs=tuple(spaces("v", "v")),
        compiler_params=pltpu.CompilerParams(vmem_limit_bytes=4 << 20),
    )(keep, got)


BESIDE = [(0, 1), (1, 0), (2, 3), (3, 2)]
BEYOND = [(0, 2), (2, 3), (3, 1), (1, 0)]
COLS = [(0, 1), (1, 0)]
CORES = [(0, 1), (1, 0), (2, 3), (3, 2)]
CHIPS = [(0, 2), (2, 0), (1, 3), (3, 1)]
MIDDLE = [(r * 4 + m, (3 - r) * 4 + m if r in (1, 2) else r * 4 + (m ^ 1)) for r in range(4) for m in range(4)]
ACROSS = [(r * 4 + m, (r ^ 1) * 4 + (m ^ 2)) for r in range(4) for m in range(4)]


def middle_shards(a_blocks, a_codes, b_blocks, b_codes):
    a_slots, slots = a_blocks.shape[0], b_blocks.shape[0]
    a_pack, b_pack, mixed, b_second = pack(a_codes, b_codes, a_blocks, b_blocks)
    b_across = lax.ppermute(b_pack, ("row", "layer"), MIDDLE)
    end_mixed = lax.ppermute(mixed, "row", BESIDE)
    far_second = lax.ppermute(b_second, "row", BEYOND)
    end_second = lax.ppermute(b_second, "row", BESIDE)
    a_other = lax.ppermute(a_pack, "col", COLS)
    end_first, a_end = part(end_mixed, end_mixed.shape[0] - a_pack.shape[0])
    far_first = lax.ppermute(end_first, ("row", "layer"), MIDDLE)
    a_end_other = lax.ppermute(a_end, "col", COLS)

    dense = early(b_pack, b_across, end_first, end_second, far_second, a_other, slots)
    dense, own_keep, own_send = own_product(
        (a_pack, a_other), dense, far_first, a_slots, slots
    )
    end_keep, end_send = end_product((a_end, a_end_other), dense, a_slots)

    def over_cores(keep, send):
        return fold(keep, lax.ppermute(send, "layer", CORES))

    own_near, own_far = over_cores(own_keep, own_send)
    end_near, end_far = over_cores(end_keep, end_send)
    out = own_near + lax.ppermute(end_near, "row", BESIDE)
    out = out + lax.ppermute(end_far, ("row", "layer"), ACROSS)
    out = out + lax.ppermute(own_far, "layer", CHIPS)
    return out.astype(jnp.bfloat16)


def solution(mesh):
    placed = (
        P(("row", "col", "layer"), None, None),
        P(("row", "col", "layer")),
        P(("row", "col", "layer"), None, None),
        P(("row", "col", "layer")),
    )
    body = middle_shards if middle_plan(mesh.shape) else shards
    return jax.shard_map(
        body, mesh=mesh, in_specs=placed, out_specs=P(("row", "layer"), "col"), check_vma=False
    )
```

```python
import functools

import jax
import jax.numpy as jnp
from jax import lax
from jax.experimental import pallas as pl
from jax.experimental.pallas import tpu as pltpu
from jax.sharding import PartitionSpec as P

RB = 4
CB = 4
KB = 6


def from_behind(block, axis, distance):
    devices = range(lax.axis_size(axis))
    route = [((i - distance) % len(devices), i) for i in devices]
    return lax.ppermute(block, axis, route)


def dense_left(block_stack, block_codes, part_index, pieces):
    block_width = block_stack.shape[1]
    is_live = block_codes >= 0
    row_of = block_codes // (pieces * KB)
    part_of = block_codes // KB % pieces
    inner_of = block_codes % KB
    selected = is_live & (part_of == part_index)
    row_hits = row_of[:, None] == jnp.arange(RB)[None, :]
    inner_hit = inner_of[:, None] == jnp.arange(KB)[None, :]
    weight = (selected[:, None, None] & row_hits[:, :, None] & inner_hit[:, None, :]).astype(
        jnp.bfloat16
    )
    dense_tile = jnp.einsum(
        "aik,axy->ixky", weight, block_stack, preferred_element_type=jnp.float32
    )
    return dense_tile.astype(jnp.bfloat16).reshape(RB * block_width, KB * block_width)


def dense_right(block_stack, block_codes):
    block_width = block_stack.shape[1]
    is_live = block_codes >= 0
    inner_of = block_codes // CB
    column_of = block_codes % CB
    inner_hit = inner_of[:, None] == jnp.arange(KB)[None, :]
    column_hit = column_of[:, None] == jnp.arange(CB)[None, :]
    weight = (is_live[:, None, None] & inner_hit[:, :, None] & column_hit[:, None, :]).astype(
        jnp.bfloat16
    )
    dense_tile = jnp.einsum(
        "skj,sxy->kxjy", weight, block_stack, preferred_element_type=jnp.float32
    )
    return dense_tile.astype(jnp.bfloat16).reshape(KB * block_width, CB * block_width)


def shards(a_blocks, a_codes, b_blocks, b_codes):
    row_count = lax.axis_size("row")
    col_count = lax.axis_size("col")
    pieces = row_count // col_count
    block_width = a_blocks.shape[1]
    row_index = lax.axis_index("row")
    col_index = lax.axis_index("col")
    a_stack, a_tags = (
        lax.all_to_all(a_blocks, "col", split_axis=0, concat_axis=0, tiled=True),
        lax.all_to_all(a_codes, "col", split_axis=0, concat_axis=0, tiled=True),
    )
    b_stack, b_tags = (
        lax.all_to_all(b_blocks, "row", split_axis=0, concat_axis=0, tiled=True),
        lax.all_to_all(b_codes, "row", split_axis=0, concat_axis=0, tiled=True),
    )

    def multiply(accumulated, left_stack, left_codes, right_stack, right_codes, piece_index):
        left_tile = dense_left(left_stack, left_codes, piece_index // col_count, pieces)
        right_tile = dense_right(right_stack, right_codes)
        return accumulated + jnp.dot(left_tile, right_tile, preferred_element_type=jnp.float32)

    start_sum = jnp.zeros((RB * block_width, CB * block_width), jnp.float32)

    def advance(visit_step, loop_state):
        accumulated, left_stack, left_codes, right_stack, right_codes = loop_state
        piece_index = (row_index + col_index + visit_step) % row_count
        accumulated = multiply(
            accumulated, left_stack, left_codes, right_stack, right_codes, piece_index
        )
        left_stack, left_codes = from_behind((left_stack, left_codes), "col", -1)
        right_stack, right_codes = from_behind((right_stack, right_codes), "row", -1)
        return (accumulated, left_stack, left_codes, right_stack, right_codes)

    loop_state = lax.fori_loop(
        0, row_count - 1, advance, (start_sum, a_stack, a_tags, b_stack, b_tags)
    )
    accumulated, left_stack, left_codes, right_stack, right_codes = loop_state
    last_piece = (row_index + col_index + row_count - 1) % row_count
    accumulated = multiply(
        accumulated, left_stack, left_codes, right_stack, right_codes, last_piece
    )
    reduced = lax.psum_scatter(accumulated, "layer", scatter_dimension=0, tiled=True)
    return reduced.astype(jnp.bfloat16)


CODE_ROWS = 16
FIRST = 8


def middle_plan(mesh_shape):
    return (mesh_shape["row"], mesh_shape["col"], mesh_shape["layer"]) == (4, 2, 4)


def spaces(*names):
    kinds = {"s": pltpu.SMEM, "v": pltpu.VMEM, "h": pltpu.HBM}
    return [pl.BlockSpec(memory_space=kinds[name]) for name in names]


def first_slots(slots):
    return slots * FIRST // 16


def pack_body(a_codes, b_codes, a_ref, b_ref, a_out, b_out, mixed_out, second_out, sems):
    a_rows, b_rows = a_ref.shape[0], b_ref.shape[0]
    width = a_ref.shape[1]
    second = second_out.shape[0] - CODE_ROWS
    first = b_rows - second
    copies = [
        pltpu.make_async_copy(b_ref, b_out.at[pl.ds(0, b_rows)], sems.at[0]),
        pltpu.make_async_copy(a_ref, a_out.at[pl.ds(0, a_rows)], sems.at[1]),
    ]
    for copy in copies:
        copy.start()

    def code_rows(codes_ref):
        lanes = lax.broadcasted_iota(jnp.int32, (CODE_ROWS, width), 1)
        values = jnp.full((CODE_ROWS, width), -1, jnp.int32)
        for slot in range(codes_ref.shape[0]):
            values = jnp.where(lanes == slot, codes_ref[slot], values)
        return values.astype(jnp.float32).astype(jnp.bfloat16)

    a_tail, b_tail = code_rows(a_codes), code_rows(b_codes)
    a_out[pl.ds(a_rows, CODE_ROWS), :] = a_tail
    b_out[pl.ds(b_rows, CODE_ROWS), :] = b_tail
    mixed_out[pl.ds(first, CODE_ROWS), :] = b_tail
    mixed_out[pl.ds(first + CODE_ROWS + a_rows, CODE_ROWS), :] = a_tail
    second_out[pl.ds(second, CODE_ROWS), :] = b_tail
    copies[0].wait()
    mixed_out[pl.ds(0, first), :] = b_out[pl.ds(0, first), :]
    second_out[pl.ds(0, second), :] = b_out[pl.ds(first, second), :]
    copies[1].wait()
    mixed_out[pl.ds(first + CODE_ROWS, a_rows), :] = a_out[pl.ds(0, a_rows), :]


def pack(a_codes, b_codes, a_blocks, b_blocks):
    width = a_blocks.shape[1]
    a_flat = a_blocks.reshape(-1, width)
    b_flat = b_blocks.reshape(-1, width)
    a_rows, b_rows = a_flat.shape[0], b_flat.shape[0]
    first = first_slots(b_blocks.shape[0]) * width
    sizes = (
        a_rows + CODE_ROWS,
        b_rows + CODE_ROWS,
        first + a_rows + 2 * CODE_ROWS,
        b_rows - first + CODE_ROWS,
    )
    return pl.pallas_call(
        pack_body,
        out_shape=tuple(jax.ShapeDtypeStruct((rows, width), jnp.bfloat16) for rows in sizes),
        in_specs=spaces("s", "s", "h", "h"),
        out_specs=tuple(spaces("v", "v", "v", "v")),
        scratch_shapes=[pltpu.SemaphoreType.DMA((2,))],
        compiler_params=pltpu.CompilerParams(vmem_limit_bytes=8 << 20),
    )(*(pltpu.with_memory_space_constraint(x, pltpu.HBM) for x in (a_codes, b_codes, a_flat, b_flat)))


def part_body(mixed, first, second):
    rows = first.shape[0]
    first[...] = mixed[pl.ds(0, rows), :]
    second[...] = mixed[pl.ds(rows, second.shape[0]), :]


def part(mixed, rows):
    sizes = (rows, mixed.shape[0] - rows)
    return pl.pallas_call(
        part_body,
        out_shape=tuple(jax.ShapeDtypeStruct((n, mixed.shape[1]), mixed.dtype) for n in sizes),
        in_specs=spaces("v"),
        out_specs=tuple(spaces("v", "v")),
        compiler_params=pltpu.CompilerParams(vmem_limit_bytes=4 << 20),
    )(mixed)


def fetch_codes(packs, staged, codes, sem):
    for index, pack_ref in enumerate(packs):
        tail = pack_ref[pl.ds(pack_ref.shape[0] - CODE_ROWS, CODE_ROWS), :]
        staged[pl.ds(index, 1), :] = tail.astype(jnp.float32).astype(jnp.int32)[:1]
    return pltpu.make_async_copy(staged, codes, sem)


def code_scratch():
    return [
        pltpu.VMEM((8, 128), jnp.int32),
        pltpu.SMEM((8, 128), jnp.int32),
        pltpu.SemaphoreType.DMA(()),
    ]


def in_middle():
    row = lax.axis_index("row")
    return jnp.logical_or(row == 1, row == 2)


def put_blocks(dense, source, codes, line, first_slot, count, slots, col):
    width = source.shape[1]
    owners = 4
    for index in range(count):
        code = codes[line, first_slot + index]

        @pl.when(code >= 0)
        def _():
            piece = lax.rem((first_slot + index) // (slots // owners) + col, owners)
            inner = piece * KB + code // CB
            column = lax.rem(code, CB)
            dense[
                pl.ds(pl.multiple_of(inner * width, width), width),
                pl.ds(pl.multiple_of(column * width, width), width),
            ] = source[pl.ds(index * width, width), :]


def early_body(slots, own, across, first, second, dense, staged, codes, sem):
    cut = first_slots(slots)

    @pl.when(in_middle())
    def _():
        col = lax.axis_index("col")
        copy = fetch_codes((own, across, first), staged, codes, sem)
        copy.start()
        dense[...] = jnp.zeros_like(dense)
        copy.wait()
        put_blocks(dense, own, codes, 0, 0, slots, slots, col)
        put_blocks(dense, across, codes, 1, 0, slots, slots, col)
        put_blocks(dense, first, codes, 2, 0, cut, slots, col)
        put_blocks(dense, second, codes, 2, cut, slots - cut, slots, col)


def early(own, across, first, second, slots):
    width = own.shape[1]
    return pl.pallas_call(
        functools.partial(early_body, slots),
        out_shape=jax.ShapeDtypeStruct((4 * KB * width, CB * width), jnp.bfloat16),
        in_specs=spaces("v", "v", "v", "v"),
        out_specs=spaces("v")[0],
        scratch_shapes=code_scratch(),
        compiler_params=pltpu.CompilerParams(vmem_limit_bytes=12 << 20),
    )(own, across, first, second)


def multiply_group(dense, total, packs, codes, slots, row):
    width = packs[0].shape[1]
    pieces, owners = 2, 2
    core = lax.rem(lax.axis_index("layer"), 2)
    total[...] = jnp.zeros_like(total)
    for source in range(2):
        for slot in range(slots):
            code = codes[source, slot]
            live = (code >= 0).astype(jnp.int32)
            safe = jnp.maximum(code, 0)
            owner = slot // (slots // owners)
            piece = lax.rem(row + owner, owners) + owners * lax.rem(safe // KB, pieces)
            inner = piece * KB + lax.rem(safe, KB)
            block_row = safe // (pieces * KB)
            sent = (lax.rem(block_row, 2) != core).astype(jnp.int32)
            spot = live * (sent * 2 + block_row // 2) + (1 - live) * 4
            part = jnp.dot(
                packs[source][pl.ds(slot * width, width), :],
                dense[pl.ds(pl.multiple_of(inner * width, width), width), :],
                preferred_element_type=jnp.float32,
            )
            total[pl.ds(pl.multiple_of(spot * width, width), width), :] += part


def end_body(a_slots, slots, packs_0, packs_1, dense_in, first, second,
             dense, keep, send, total, staged, codes, sem):
    cut = first_slots(slots)
    rows = keep.shape[0]
    del dense_in

    @pl.when(jnp.logical_not(in_middle()))
    def _():
        keep[...] = jnp.zeros_like(keep)
        send[...] = jnp.zeros_like(send)

    @pl.when(in_middle())
    def _():
        copy = fetch_codes((packs_0, packs_1, first), staged, codes, sem)
        copy.start()
        copy.wait()
        col = lax.axis_index("col")
        put_blocks(dense, first, codes, 2, 0, cut, slots, col)
        put_blocks(dense, second, codes, 2, cut, slots - cut, slots, col)
        row = jnp.where(lax.axis_index("row") == 1, 0, 3)
        multiply_group(dense, total, (packs_0, packs_1), codes, a_slots, row)
        keep[...] = total[pl.ds(0, rows), :]
        send[...] = total[pl.ds(rows, rows), :]


def own_body(a_slots, packs_0, packs_1, dense, keep, send, total, staged, codes, sem):
    rows = keep.shape[0]

    @pl.when(jnp.logical_not(in_middle()))
    def _():
        keep[...] = jnp.zeros_like(keep)
        send[...] = jnp.zeros_like(send)

    @pl.when(in_middle())
    def _():
        copy = fetch_codes((packs_0, packs_1), staged, codes, sem)
        copy.start()
        copy.wait()
        multiply_group(dense, total, (packs_0, packs_1), codes, a_slots, lax.axis_index("row"))
        keep[...] = total[pl.ds(0, rows), :]
        send[...] = total[pl.ds(rows, rows), :]


def end_product(packs, dense, first, second, a_slots, slots):
    width = packs[0].shape[1]
    half = jax.ShapeDtypeStruct((2 * width, CB * width), jnp.float32)
    return pl.pallas_call(
        functools.partial(end_body, a_slots, slots),
        out_shape=(jax.ShapeDtypeStruct(dense.shape, dense.dtype), half, half),
        in_specs=spaces("v", "v", "v", "v", "v"),
        out_specs=tuple(spaces("v", "v", "v")),
        scratch_shapes=[pltpu.VMEM((5 * width, CB * width), jnp.float32)] + code_scratch(),
        input_output_aliases={2: 0},
        compiler_params=pltpu.CompilerParams(vmem_limit_bytes=16 << 20),
    )(*packs, dense, first, second)


def own_product(packs, dense, a_slots):
    width = packs[0].shape[1]
    half = jax.ShapeDtypeStruct((2 * width, CB * width), jnp.float32)
    return pl.pallas_call(
        functools.partial(own_body, a_slots),
        out_shape=(half, half),
        in_specs=spaces("v", "v", "v"),
        out_specs=tuple(spaces("v", "v")),
        scratch_shapes=[pltpu.VMEM((5 * width, CB * width), jnp.float32)] + code_scratch(),
        compiler_params=pltpu.CompilerParams(vmem_limit_bytes=16 << 20),
    )(*packs, dense)


def fold_body(keep, got, near, far):
    rows = near.shape[0]
    chip = lax.axis_index("layer") // 2
    for out, index in ((near, chip), (far, 1 - chip)):
        block = pl.ds(pl.multiple_of(index * rows, rows), rows)
        out[...] = keep[block, :] + got[block, :]


def fold(keep, got):
    rows, width = keep.shape
    half = jax.ShapeDtypeStruct((rows // 2, width), keep.dtype)
    return pl.pallas_call(
        fold_body,
        out_shape=(half, half),
        in_specs=spaces("v", "v"),
        out_specs=tuple(spaces("v", "v")),
        compiler_params=pltpu.CompilerParams(vmem_limit_bytes=4 << 20),
    )(keep, got)


BESIDE = [(0, 1), (1, 0), (2, 3), (3, 2)]
BEYOND = [(0, 2), (2, 3), (3, 1), (1, 0)]
COLS = [(0, 1), (1, 0)]
CORES = [(0, 1), (1, 0), (2, 3), (3, 2)]
EVERY = [(r, m) for r in range(4) for m in range(4)]
MIDDLE = [(r * 4 + m, (3 - r) * 4 + m if r in (1, 2) else r * 4 + (m ^ 1)) for r, m in EVERY]
CHIPS = [(r * 4 + m, r * 4 + (m ^ 2 if r in (1, 2) else m ^ 1)) for r, m in EVERY]
ACROSS = [(r * 4 + m, (r ^ 1) * 4 + (m ^ 2 if r in (1, 2) else m)) for r, m in EVERY]


def middle_shards(a_blocks, a_codes, b_blocks, b_codes):
    a_slots, slots = a_blocks.shape[0], b_blocks.shape[0]
    a_pack, b_pack, mixed, b_second = pack(a_codes, b_codes, a_blocks, b_blocks)
    b_across = lax.ppermute(b_pack, ("row", "layer"), MIDDLE)
    end_mixed = lax.ppermute(mixed, "row", BESIDE)
    far_second = lax.ppermute(b_second, "row", BEYOND)
    end_second = lax.ppermute(b_second, "row", BESIDE)
    a_other = lax.ppermute(a_pack, "col", COLS)
    end_first, a_end = part(end_mixed, end_mixed.shape[0] - a_pack.shape[0])
    far_first = lax.ppermute(end_first, ("row", "layer"), MIDDLE)
    a_end, a_other = lax.optimization_barrier((a_end, a_other))
    a_end_other = lax.ppermute(a_end, "col", COLS)

    dense = early(b_pack, b_across, end_first, end_second, slots)
    dense, end_keep, end_send = end_product(
        (a_end, a_end_other), dense, far_first, far_second, a_slots, slots
    )
    own_keep, own_send = own_product((a_pack, a_other), dense, a_slots)

    def over_cores(keep, send):
        return fold(keep, lax.ppermute(send, "layer", CORES))

    end_near, end_far = over_cores(end_keep, end_send)
    own_send, _ = lax.optimization_barrier((own_send, end_near))
    own_near, own_far = over_cores(own_keep, own_send)
    out = own_near + lax.ppermute(end_near, "row", BESIDE)
    out = out + lax.ppermute(end_far, ("row", "layer"), ACROSS)
    out = out + lax.ppermute(own_far, ("row", "layer"), CHIPS)
    return out.astype(jnp.bfloat16)


def solution(mesh):
    placed = (
        P(("row", "col", "layer"), None, None),
        P(("row", "col", "layer")),
        P(("row", "col", "layer"), None, None),
        P(("row", "col", "layer")),
    )
    body = middle_shards if middle_plan(mesh.shape) else shards
    return jax.shard_map(
        body, mesh=mesh, in_specs=placed, out_specs=P(("row", "layer"), "col"), check_vma=False
    )
```

```python
import functools

import jax
import jax.numpy as jnp
from jax import lax
from jax.experimental import pallas as pl
from jax.experimental.pallas import tpu as pltpu
from jax.sharding import PartitionSpec as P

RB = 4
CB = 4
KB = 6


def from_behind(block, axis, distance):
    devices = range(lax.axis_size(axis))
    route = [((i - distance) % len(devices), i) for i in devices]
    return lax.ppermute(block, axis, route)


def dense_left(block_stack, block_codes, part_index, pieces):
    block_width = block_stack.shape[1]
    is_live = block_codes >= 0
    row_of = block_codes // (pieces * KB)
    part_of = block_codes // KB % pieces
    inner_of = block_codes % KB
    selected = is_live & (part_of == part_index)
    row_hits = row_of[:, None] == jnp.arange(RB)[None, :]
    inner_hit = inner_of[:, None] == jnp.arange(KB)[None, :]
    weight = (selected[:, None, None] & row_hits[:, :, None] & inner_hit[:, None, :]).astype(
        jnp.bfloat16
    )
    dense_tile = jnp.einsum(
        "aik,axy->ixky", weight, block_stack, preferred_element_type=jnp.float32
    )
    return dense_tile.astype(jnp.bfloat16).reshape(RB * block_width, KB * block_width)


def dense_right(block_stack, block_codes):
    block_width = block_stack.shape[1]
    is_live = block_codes >= 0
    inner_of = block_codes // CB
    column_of = block_codes % CB
    inner_hit = inner_of[:, None] == jnp.arange(KB)[None, :]
    column_hit = column_of[:, None] == jnp.arange(CB)[None, :]
    weight = (is_live[:, None, None] & inner_hit[:, :, None] & column_hit[:, None, :]).astype(
        jnp.bfloat16
    )
    dense_tile = jnp.einsum(
        "skj,sxy->kxjy", weight, block_stack, preferred_element_type=jnp.float32
    )
    return dense_tile.astype(jnp.bfloat16).reshape(KB * block_width, CB * block_width)


def shards(a_blocks, a_codes, b_blocks, b_codes):
    row_count = lax.axis_size("row")
    col_count = lax.axis_size("col")
    pieces = row_count // col_count
    block_width = a_blocks.shape[1]
    row_index = lax.axis_index("row")
    col_index = lax.axis_index("col")
    a_stack, a_tags = (
        lax.all_to_all(a_blocks, "col", split_axis=0, concat_axis=0, tiled=True),
        lax.all_to_all(a_codes, "col", split_axis=0, concat_axis=0, tiled=True),
    )
    b_stack, b_tags = (
        lax.all_to_all(b_blocks, "row", split_axis=0, concat_axis=0, tiled=True),
        lax.all_to_all(b_codes, "row", split_axis=0, concat_axis=0, tiled=True),
    )

    def multiply(accumulated, left_stack, left_codes, right_stack, right_codes, piece_index):
        left_tile = dense_left(left_stack, left_codes, piece_index // col_count, pieces)
        right_tile = dense_right(right_stack, right_codes)
        return accumulated + jnp.dot(left_tile, right_tile, preferred_element_type=jnp.float32)

    start_sum = jnp.zeros((RB * block_width, CB * block_width), jnp.float32)

    def advance(visit_step, loop_state):
        accumulated, left_stack, left_codes, right_stack, right_codes = loop_state
        piece_index = (row_index + col_index + visit_step) % row_count
        accumulated = multiply(
            accumulated, left_stack, left_codes, right_stack, right_codes, piece_index
        )
        left_stack, left_codes = from_behind((left_stack, left_codes), "col", -1)
        right_stack, right_codes = from_behind((right_stack, right_codes), "row", -1)
        return (accumulated, left_stack, left_codes, right_stack, right_codes)

    loop_state = lax.fori_loop(
        0, row_count - 1, advance, (start_sum, a_stack, a_tags, b_stack, b_tags)
    )
    accumulated, left_stack, left_codes, right_stack, right_codes = loop_state
    last_piece = (row_index + col_index + row_count - 1) % row_count
    accumulated = multiply(
        accumulated, left_stack, left_codes, right_stack, right_codes, last_piece
    )
    reduced = lax.psum_scatter(accumulated, "layer", scatter_dimension=0, tiled=True)
    return reduced.astype(jnp.bfloat16)


CODE_ROWS = 16
FIRST = 8
CUT = 2


def middle_plan(mesh_shape):
    return (mesh_shape["row"], mesh_shape["col"], mesh_shape["layer"]) == (4, 2, 4)


def spaces(*names):
    kinds = {"s": pltpu.SMEM, "v": pltpu.VMEM, "h": pltpu.HBM}
    return [pl.BlockSpec(memory_space=kinds[name]) for name in names]


def first_slots(slots):
    return slots * FIRST // 16


def pack_body(a_codes, b_codes, a_ref, b_ref, a_out, b_out, mixed_out, second_out, sems):
    a_rows, b_rows = a_ref.shape[0], b_ref.shape[0]
    width = a_ref.shape[1]
    second = second_out.shape[0] - CODE_ROWS
    first = b_rows - second
    copies = [
        pltpu.make_async_copy(b_ref, b_out.at[pl.ds(0, b_rows)], sems.at[0]),
        pltpu.make_async_copy(a_ref, a_out.at[pl.ds(0, a_rows)], sems.at[1]),
    ]
    for copy in copies:
        copy.start()

    def code_rows(codes_ref):
        lanes = lax.broadcasted_iota(jnp.int32, (CODE_ROWS, width), 1)
        values = jnp.full((CODE_ROWS, width), -1, jnp.int32)
        for slot in range(codes_ref.shape[0]):
            values = jnp.where(lanes == slot, codes_ref[slot], values)
        return values.astype(jnp.float32).astype(jnp.bfloat16)

    a_tail, b_tail = code_rows(a_codes), code_rows(b_codes)
    a_out[pl.ds(a_rows, CODE_ROWS), :] = a_tail
    b_out[pl.ds(b_rows, CODE_ROWS), :] = b_tail
    mixed_out[pl.ds(first, CODE_ROWS), :] = b_tail
    mixed_out[pl.ds(first + CODE_ROWS + a_rows, CODE_ROWS), :] = a_tail
    second_out[pl.ds(second, CODE_ROWS), :] = b_tail
    copies[0].wait()
    mixed_out[pl.ds(0, first), :] = b_out[pl.ds(0, first), :]
    second_out[pl.ds(0, second), :] = b_out[pl.ds(first, second), :]
    copies[1].wait()
    mixed_out[pl.ds(first + CODE_ROWS, a_rows), :] = a_out[pl.ds(0, a_rows), :]


def pack(a_codes, b_codes, a_blocks, b_blocks):
    width = a_blocks.shape[1]
    a_flat = a_blocks.reshape(-1, width)
    b_flat = b_blocks.reshape(-1, width)
    a_rows, b_rows = a_flat.shape[0], b_flat.shape[0]
    first = first_slots(b_blocks.shape[0]) * width
    sizes = (
        a_rows + CODE_ROWS,
        b_rows + CODE_ROWS,
        first + a_rows + 2 * CODE_ROWS,
        b_rows - first + CODE_ROWS,
    )
    return pl.pallas_call(
        pack_body,
        out_shape=tuple(jax.ShapeDtypeStruct((rows, width), jnp.bfloat16) for rows in sizes),
        in_specs=spaces("s", "s", "h", "h"),
        out_specs=tuple(spaces("v", "v", "v", "v")),
        scratch_shapes=[pltpu.SemaphoreType.DMA((2,))],
        compiler_params=pltpu.CompilerParams(vmem_limit_bytes=8 << 20),
    )(*(pltpu.with_memory_space_constraint(x, pltpu.HBM) for x in (a_codes, b_codes, a_flat, b_flat)))


def part_body(mixed, first, second):
    rows = first.shape[0]
    first[...] = mixed[pl.ds(0, rows), :]
    second[...] = mixed[pl.ds(rows, second.shape[0]), :]


def part(mixed, rows):
    sizes = (rows, mixed.shape[0] - rows)
    return pl.pallas_call(
        part_body,
        out_shape=tuple(jax.ShapeDtypeStruct((n, mixed.shape[1]), mixed.dtype) for n in sizes),
        in_specs=spaces("v"),
        out_specs=tuple(spaces("v", "v")),
        compiler_params=pltpu.CompilerParams(vmem_limit_bytes=4 << 20),
    )(mixed)


def fetch_codes(packs, staged, codes, sem):
    for index, pack_ref in enumerate(packs):
        tail = pack_ref[pl.ds(pack_ref.shape[0] - CODE_ROWS, CODE_ROWS), :]
        staged[pl.ds(index, 1), :] = tail.astype(jnp.float32).astype(jnp.int32)[:1]
    return pltpu.make_async_copy(staged, codes, sem)


def code_scratch():
    return [
        pltpu.VMEM((8, 128), jnp.int32),
        pltpu.SMEM((8, 128), jnp.int32),
        pltpu.SemaphoreType.DMA(()),
    ]


def in_middle():
    row = lax.axis_index("row")
    return jnp.logical_or(row == 1, row == 2)


def put_blocks(dense, source, codes, line, first_slot, count, slots, col):
    width = source.shape[1]
    owners = 4
    for index in range(count):
        code = codes[line, first_slot + index]

        @pl.when(code >= 0)
        def _():
            piece = lax.rem((first_slot + index) // (slots // owners) + col, owners)
            inner = piece * KB + code // CB
            column = lax.rem(code, CB)
            dense[
                pl.ds(pl.multiple_of(inner * width, width), width),
                pl.ds(pl.multiple_of(column * width, width), width),
            ] = source[pl.ds(index * width, width), :]


def early_body(slots, own, across, first, second, dense, staged, codes, sem):
    cut = first_slots(slots)

    @pl.when(in_middle())
    def _():
        col = lax.axis_index("col")
        copy = fetch_codes((own, across, first), staged, codes, sem)
        copy.start()
        dense[...] = jnp.zeros_like(dense)
        copy.wait()
        put_blocks(dense, own, codes, 0, 0, slots, slots, col)
        put_blocks(dense, across, codes, 1, 0, slots, slots, col)
        put_blocks(dense, first, codes, 2, 0, cut, slots, col)
        put_blocks(dense, second, codes, 2, cut, slots - cut, slots, col)


def early(own, across, first, second, slots):
    width = own.shape[1]
    return pl.pallas_call(
        functools.partial(early_body, slots),
        out_shape=jax.ShapeDtypeStruct((4 * KB * width, CB * width), jnp.bfloat16),
        in_specs=spaces("v", "v", "v", "v"),
        out_specs=spaces("v")[0],
        scratch_shapes=code_scratch(),
        compiler_params=pltpu.CompilerParams(vmem_limit_bytes=12 << 20),
    )(own, across, first, second)


def multiply_group(dense, total, packs, codes, line, slots, row):
    width = packs[0].shape[1]
    pieces, owners = 2, 2
    core = lax.rem(lax.axis_index("layer"), 2)
    for source in range(2):
        for slot in range(slots):
            code = codes[line + source, slot]
            live = (code >= 0).astype(jnp.int32)
            safe = jnp.maximum(code, 0)
            owner = slot // (slots // owners)
            piece = lax.rem(row + owner, owners) + owners * lax.rem(safe // KB, pieces)
            inner = piece * KB + lax.rem(safe, KB)
            block_row = safe // (pieces * KB)
            sent = (lax.rem(block_row, 2) != core).astype(jnp.int32)
            spot = live * (sent * 2 + block_row // 2) + (1 - live) * 4
            part = jnp.dot(
                packs[source][pl.ds(slot * width, width), :],
                dense[pl.ds(pl.multiple_of(inner * width, width), width), :],
                preferred_element_type=jnp.float32,
            )
            total[pl.ds(pl.multiple_of(spot * width, width), width), :] += part


def product_body(a_slots, slots, first_column, own_0, own_1, end_0, end_1, dense_in, first, second,
                 dense, keep, send, total, staged, codes, sem):
    cut = first_slots(slots)
    rows, columns = keep.shape[0] // 2, keep.shape[1]
    place = first_column > 0
    del dense_in

    @pl.when(jnp.logical_not(in_middle()))
    def _():
        keep[...] = jnp.zeros_like(keep)
        send[...] = jnp.zeros_like(send)

    @pl.when(in_middle())
    def _():
        copy = fetch_codes((end_0, end_1, own_0, own_1, first), staged, codes, sem)
        copy.start()
        total[...] = jnp.zeros_like(total)
        copy.wait()
        col, row = lax.axis_index("col"), lax.axis_index("row")
        if place:
            put_blocks(dense, first, codes, 4, 0, cut, slots, col)
            put_blocks(dense, second, codes, 4, cut, slots - cut, slots, col)
        next_row = jnp.where(row == 1, 0, 3)
        part = dense.at[:, pl.ds(first_column, columns)]
        multiply_group(part, total.at[0], (end_0, end_1), codes, 0, a_slots, next_row)
        multiply_group(part, total.at[1], (own_0, own_1), codes, 2, a_slots, row)
        for group in range(2):
            keep[pl.ds(group * rows, rows), :] = total[group, pl.ds(0, rows), :]
            send[pl.ds(group * rows, rows), :] = total[group, pl.ds(rows, rows), :]


def product(own, end, dense, first, second, first_column, columns, a_slots, slots):
    width = own[0].shape[1]
    half = jax.ShapeDtypeStruct((4 * width, columns), jnp.float32)
    return pl.pallas_call(
        functools.partial(product_body, a_slots, slots, first_column),
        out_shape=(jax.ShapeDtypeStruct(dense.shape, dense.dtype), half, half),
        in_specs=spaces(*"vvvvvvv"),
        out_specs=tuple(spaces(*"vvv")),
        scratch_shapes=[pltpu.VMEM((2, 5 * width, columns), jnp.float32)] + code_scratch(),
        input_output_aliases={4: 0},
        compiler_params=pltpu.CompilerParams(vmem_limit_bytes=20 << 20),
    )(*own, *end, dense, first, second)


def fold_body(keep, got, end_near, end_far, own_near, own_far):
    rows = end_near.shape[0]
    chip = lax.axis_index("layer") // 2
    for first, near, far in ((0, end_near, end_far), (2 * rows, own_near, own_far)):
        for out, index in ((near, chip), (far, 1 - chip)):
            block = pl.ds(pl.multiple_of(first + index * rows, rows), rows)
            out[...] = keep[block, :] + got[block, :]


def fold(keep, got):
    part = jax.ShapeDtypeStruct((keep.shape[0] // 4, keep.shape[1]), jnp.float32)
    return pl.pallas_call(
        fold_body,
        out_shape=(part,) * 4,
        in_specs=spaces(*"vv"),
        out_specs=tuple(spaces(*"vvvv")),
        compiler_params=pltpu.CompilerParams(vmem_limit_bytes=8 << 20),
    )(keep, got)


def settle_body(near, got, out):
    out[...] = (near[...] + got[...]).astype(out.dtype)


def settle(near, got):
    return pl.pallas_call(
        settle_body,
        out_shape=jax.ShapeDtypeStruct(near.shape, jnp.bfloat16),
        in_specs=spaces("v", "v"),
        out_specs=spaces("v")[0],
        compiler_params=pltpu.CompilerParams(vmem_limit_bytes=4 << 20),
    )(near, got)


def finish_body(left, left_got, right, right_got, near, far, settled, out):
    cut = left.shape[1]
    out[:, pl.ds(0, cut)] = ((left[...] + left_got[...]) + (near[...] + far[...])).astype(out.dtype)
    rest = (right[...] + right_got[...]) + settled[...].astype(jnp.float32)
    out[:, pl.ds(cut, rest.shape[1])] = rest.astype(out.dtype)


def finish(*parts):
    shape = (parts[0].shape[0], parts[0].shape[1] + parts[2].shape[1])
    return pl.pallas_call(
        finish_body,
        out_shape=jax.ShapeDtypeStruct(shape, jnp.bfloat16),
        in_specs=spaces(*"vvvvvvv"),
        out_specs=spaces("v")[0],
        compiler_params=pltpu.CompilerParams(vmem_limit_bytes=4 << 20),
    )(*parts)


BESIDE = [(0, 1), (1, 0), (2, 3), (3, 2)]
BEYOND = [(0, 2), (2, 3), (3, 1), (1, 0)]
COLS = [(0, 1), (1, 0)]
CORES = [(0, 1), (1, 0), (2, 3), (3, 2)]
EVERY = [(r, m) for r in range(4) for m in range(4)]
MIDDLE = [(r * 4 + m, (3 - r) * 4 + m if r in (1, 2) else r * 4 + (m ^ 1)) for r, m in EVERY]
CHIPS = [(r * 4 + m, r * 4 + (m ^ 2 if r in (1, 2) else m ^ 1)) for r, m in EVERY]
ACROSS = [(r * 4 + m, (r ^ 1) * 4 + (m ^ 2 if r in (1, 2) else m)) for r, m in EVERY]


def middle_shards(a_blocks, a_codes, b_blocks, b_codes):
    a_slots, slots = a_blocks.shape[0], b_blocks.shape[0]
    a_pack, b_pack, mixed, b_second = pack(a_codes, b_codes, a_blocks, b_blocks)
    b_across = lax.ppermute(b_pack, ("row", "layer"), MIDDLE)
    end_mixed = lax.ppermute(mixed, "row", BESIDE)
    far_second = lax.ppermute(b_second, "row", BEYOND)
    a_other = lax.ppermute(a_pack, "col", COLS)
    b_late, a_other = lax.optimization_barrier((b_second, a_other))
    end_second = lax.ppermute(b_late, "row", BESIDE)
    end_first, a_end = part(end_mixed, end_mixed.shape[0] - a_pack.shape[0])
    far_first = lax.ppermute(end_first, ("row", "layer"), MIDDLE)
    a_end, a_other = lax.optimization_barrier((a_end, a_other))
    a_end_other = lax.ppermute(a_end, "col", COLS)

    dense = early(b_pack, b_across, end_first, end_second, slots)
    columns = CB * a_blocks.shape[1]
    cut = columns * CUT // 4
    own, end = (a_pack, a_other), (a_end, a_end_other)
    dense, keep, send = product(own, end, dense, far_first, far_second, cut, columns - cut, a_slots, slots)
    got = lax.ppermute(send, "layer", CORES)
    _, left_keep, left_send = product(own, end, dense, far_first, far_second, 0, cut, a_slots, slots)
    left_got = lax.ppermute(left_send, "layer", CORES)
    rest_near, rest_far, right, right_far = fold(keep, got)
    rest_got = lax.ppermute(rest_far, ("row", "layer"), CHIPS)
    settled = lax.ppermute(settle(rest_near, rest_got), "row", BESIDE)
    right_got = lax.ppermute(right_far, ("row", "layer"), CHIPS)
    near, far, left, left_far = fold(left_keep, left_got)
    got_near = lax.ppermute(near, "row", BESIDE)
    got_far = lax.ppermute(far, ("row", "layer"), ACROSS)
    left_got = lax.ppermute(left_far, ("row", "layer"), CHIPS)
    return finish(left, left_got, right, right_got, got_near, got_far, settled)


def solution(mesh):
    placed = (
        P(("row", "col", "layer"), None, None),
        P(("row", "col", "layer")),
        P(("row", "col", "layer"), None, None),
        P(("row", "col", "layer")),
    )
    body = middle_shards if middle_plan(mesh.shape) else shards
    return jax.shard_map(
        body, mesh=mesh, in_specs=placed, out_specs=P(("row", "layer"), "col"), check_vma=False
    )
```

```python
import functools

import jax
import jax.numpy as jnp
from jax import lax
from jax.experimental import pallas as pl
from jax.experimental.pallas import tpu as pltpu
from jax.sharding import PartitionSpec as P

RB = 4
CB = 4
KB = 6


def from_behind(block, axis, distance):
    devices = range(lax.axis_size(axis))
    route = [((i - distance) % len(devices), i) for i in devices]
    return lax.ppermute(block, axis, route)


def dense_left(block_stack, block_codes, part_index, pieces):
    block_width = block_stack.shape[1]
    is_live = block_codes >= 0
    row_of = block_codes // (pieces * KB)
    part_of = block_codes // KB % pieces
    inner_of = block_codes % KB
    selected = is_live & (part_of == part_index)
    row_hits = row_of[:, None] == jnp.arange(RB)[None, :]
    inner_hit = inner_of[:, None] == jnp.arange(KB)[None, :]
    weight = (selected[:, None, None] & row_hits[:, :, None] & inner_hit[:, None, :]).astype(
        jnp.bfloat16
    )
    dense_tile = jnp.einsum(
        "aik,axy->ixky", weight, block_stack, preferred_element_type=jnp.float32
    )
    return dense_tile.astype(jnp.bfloat16).reshape(RB * block_width, KB * block_width)


def dense_right(block_stack, block_codes):
    block_width = block_stack.shape[1]
    is_live = block_codes >= 0
    inner_of = block_codes // CB
    column_of = block_codes % CB
    inner_hit = inner_of[:, None] == jnp.arange(KB)[None, :]
    column_hit = column_of[:, None] == jnp.arange(CB)[None, :]
    weight = (is_live[:, None, None] & inner_hit[:, :, None] & column_hit[:, None, :]).astype(
        jnp.bfloat16
    )
    dense_tile = jnp.einsum(
        "skj,sxy->kxjy", weight, block_stack, preferred_element_type=jnp.float32
    )
    return dense_tile.astype(jnp.bfloat16).reshape(KB * block_width, CB * block_width)


def shards(a_blocks, a_codes, b_blocks, b_codes):
    row_count = lax.axis_size("row")
    col_count = lax.axis_size("col")
    pieces = row_count // col_count
    block_width = a_blocks.shape[1]
    row_index = lax.axis_index("row")
    col_index = lax.axis_index("col")
    a_stack, a_tags = (
        lax.all_to_all(a_blocks, "col", split_axis=0, concat_axis=0, tiled=True),
        lax.all_to_all(a_codes, "col", split_axis=0, concat_axis=0, tiled=True),
    )
    b_stack, b_tags = (
        lax.all_to_all(b_blocks, "row", split_axis=0, concat_axis=0, tiled=True),
        lax.all_to_all(b_codes, "row", split_axis=0, concat_axis=0, tiled=True),
    )

    def multiply(accumulated, left_stack, left_codes, right_stack, right_codes, piece_index):
        left_tile = dense_left(left_stack, left_codes, piece_index // col_count, pieces)
        right_tile = dense_right(right_stack, right_codes)
        return accumulated + jnp.dot(left_tile, right_tile, preferred_element_type=jnp.float32)

    start_sum = jnp.zeros((RB * block_width, CB * block_width), jnp.float32)

    def advance(visit_step, loop_state):
        accumulated, left_stack, left_codes, right_stack, right_codes = loop_state
        piece_index = (row_index + col_index + visit_step) % row_count
        accumulated = multiply(
            accumulated, left_stack, left_codes, right_stack, right_codes, piece_index
        )
        left_stack, left_codes = from_behind((left_stack, left_codes), "col", -1)
        right_stack, right_codes = from_behind((right_stack, right_codes), "row", -1)
        return (accumulated, left_stack, left_codes, right_stack, right_codes)

    loop_state = lax.fori_loop(
        0, row_count - 1, advance, (start_sum, a_stack, a_tags, b_stack, b_tags)
    )
    accumulated, left_stack, left_codes, right_stack, right_codes = loop_state
    last_piece = (row_index + col_index + row_count - 1) % row_count
    accumulated = multiply(
        accumulated, left_stack, left_codes, right_stack, right_codes, last_piece
    )
    reduced = lax.psum_scatter(accumulated, "layer", scatter_dimension=0, tiled=True)
    return reduced.astype(jnp.bfloat16)


CODE_ROWS = 16
FIRST = 8
CUT = 2


def middle_plan(mesh_shape):
    return (mesh_shape["row"], mesh_shape["col"], mesh_shape["layer"]) == (4, 2, 4)


def spaces(*names):
    kinds = {"s": pltpu.SMEM, "v": pltpu.VMEM, "h": pltpu.HBM}
    return [pl.BlockSpec(memory_space=kinds[name]) for name in names]


def first_slots(slots):
    return slots * FIRST // 16


def pack_body(a_codes, b_codes, a_ref, b_ref, a_out, b_out, mixed_out, second_out, sems):
    a_rows, b_rows = a_ref.shape[0], b_ref.shape[0]
    width = a_ref.shape[1]
    second = second_out.shape[0] - CODE_ROWS
    first = b_rows - second
    copies = [
        pltpu.make_async_copy(b_ref, b_out.at[pl.ds(0, b_rows)], sems.at[0]),
        pltpu.make_async_copy(a_ref, a_out.at[pl.ds(0, a_rows)], sems.at[1]),
    ]
    for copy in copies:
        copy.start()

    def code_rows(codes_ref):
        lanes = lax.broadcasted_iota(jnp.int32, (CODE_ROWS, width), 1)
        values = jnp.full((CODE_ROWS, width), -1, jnp.int32)
        for slot in range(codes_ref.shape[0]):
            values = jnp.where(lanes == slot, codes_ref[slot], values)
        return values.astype(jnp.float32).astype(jnp.bfloat16)

    a_tail, b_tail = code_rows(a_codes), code_rows(b_codes)
    a_out[pl.ds(a_rows, CODE_ROWS), :] = a_tail
    for index in range(3):
        b_out[pl.ds(b_rows + index * CODE_ROWS, CODE_ROWS), :] = b_tail
    mixed_out[pl.ds(first, CODE_ROWS), :] = b_tail
    mixed_out[pl.ds(first + CODE_ROWS + a_rows, CODE_ROWS), :] = a_tail
    second_out[pl.ds(second, CODE_ROWS), :] = b_tail
    copies[0].wait()
    mixed_out[pl.ds(0, first), :] = b_out[pl.ds(0, first), :]
    second_out[pl.ds(0, second), :] = b_out[pl.ds(first, second), :]
    copies[1].wait()
    mixed_out[pl.ds(first + CODE_ROWS, a_rows), :] = a_out[pl.ds(0, a_rows), :]


def pack(a_codes, b_codes, a_blocks, b_blocks):
    width = a_blocks.shape[1]
    a_flat = a_blocks.reshape(-1, width)
    b_flat = b_blocks.reshape(-1, width)
    a_rows, b_rows = a_flat.shape[0], b_flat.shape[0]
    first = first_slots(b_blocks.shape[0]) * width
    sizes = (
        a_rows + CODE_ROWS,
        b_rows + 3 * CODE_ROWS,
        first + a_rows + 2 * CODE_ROWS,
        b_rows - first + CODE_ROWS,
    )
    return pl.pallas_call(
        pack_body,
        out_shape=tuple(jax.ShapeDtypeStruct((rows, width), jnp.bfloat16) for rows in sizes),
        in_specs=spaces("s", "s", "h", "h"),
        out_specs=tuple(spaces("v", "v", "v", "v")),
        scratch_shapes=[pltpu.SemaphoreType.DMA((2,))],
        compiler_params=pltpu.CompilerParams(vmem_limit_bytes=8 << 20),
    )(*(pltpu.with_memory_space_constraint(x, pltpu.HBM) for x in (a_codes, b_codes, a_flat, b_flat)))


def part_body(mixed, first, second):
    rows = first.shape[0]
    first[...] = mixed[pl.ds(0, rows), :]
    second[...] = mixed[pl.ds(rows, second.shape[0]), :]


def part(mixed, rows):
    sizes = (rows, mixed.shape[0] - rows)
    return pl.pallas_call(
        part_body,
        out_shape=tuple(jax.ShapeDtypeStruct((n, mixed.shape[1]), mixed.dtype) for n in sizes),
        in_specs=spaces("v"),
        out_specs=tuple(spaces("v", "v")),
        compiler_params=pltpu.CompilerParams(vmem_limit_bytes=4 << 20),
    )(mixed)


def fetch_codes(packs, staged, codes, sem):
    for index, pack_ref in enumerate(packs):
        tail = pack_ref[pl.ds(pack_ref.shape[0] - CODE_ROWS, CODE_ROWS), :]
        staged[pl.ds(index, 1), :] = tail.astype(jnp.float32).astype(jnp.int32)[:1]
    return pltpu.make_async_copy(staged, codes, sem)


def code_scratch():
    return [
        pltpu.VMEM((8, 128), jnp.int32),
        pltpu.SMEM((8, 128), jnp.int32),
        pltpu.SemaphoreType.DMA(()),
    ]


def in_middle():
    row = lax.axis_index("row")
    return jnp.logical_or(row == 1, row == 2)


def put_blocks(dense, source, codes, line, first_slot, count, slots, col):
    width = source.shape[1]
    owners = 4
    for index in range(count):
        code = codes[line, first_slot + index]

        @pl.when(code >= 0)
        def _():
            piece = lax.rem((first_slot + index) // (slots // owners) + col, owners)
            inner = piece * KB + code // CB
            column = lax.rem(code, CB)
            dense[
                pl.ds(pl.multiple_of(inner * width, width), width),
                pl.ds(pl.multiple_of(column * width, width), width),
            ] = source[pl.ds(index * width, width), :]


def early_body(slots, own, across, first, dense, staged, codes, sem):
    cut = first_slots(slots)

    @pl.when(in_middle())
    def _():
        col = lax.axis_index("col")
        copy = fetch_codes((own, across, first), staged, codes, sem)
        copy.start()
        dense[...] = jnp.zeros_like(dense)
        copy.wait()
        put_blocks(dense, own, codes, 0, 0, slots, slots, col)
        put_blocks(dense, across, codes, 1, 0, slots, slots, col)
        put_blocks(dense, first, codes, 2, 0, cut, slots, col)


def early(own, across, first, slots):
    width = own.shape[1]
    return pl.pallas_call(
        functools.partial(early_body, slots),
        out_shape=jax.ShapeDtypeStruct((4 * KB * width, CB * width), jnp.bfloat16),
        in_specs=spaces("v", "v", "v"),
        out_specs=spaces("v")[0],
        scratch_shapes=code_scratch(),
        compiler_params=pltpu.CompilerParams(vmem_limit_bytes=12 << 20),
    )(own, across, first)


def multiply_group(dense, total, packs, codes, line, slots, row):
    width = packs[0].shape[1]
    pieces, owners = 2, 2
    core = lax.rem(lax.axis_index("layer"), 2)
    for source in range(2):
        for slot in range(slots):
            code = codes[line + source, slot]
            live = (code >= 0).astype(jnp.int32)
            safe = jnp.maximum(code, 0)
            owner = slot // (slots // owners)
            piece = lax.rem(row + owner, owners) + owners * lax.rem(safe // KB, pieces)
            inner = piece * KB + lax.rem(safe, KB)
            block_row = safe // (pieces * KB)
            sent = (lax.rem(block_row, 2) != core).astype(jnp.int32)
            spot = live * (sent * 2 + block_row // 2) + (1 - live) * 4
            part = jnp.dot(
                packs[source][pl.ds(slot * width, width), :],
                dense[pl.ds(pl.multiple_of(inner * width, width), width), :],
                preferred_element_type=jnp.float32,
            )
            total[pl.ds(pl.multiple_of(spot * width, width), width), :] += part


def product_body(a_slots, slots, first_column, own_0, own_1, end_0, end_1, dense_in, first, second, beside,
                 dense, keep, send, total, staged, codes, sem):
    cut = first_slots(slots)
    rows, columns = keep.shape[0] // 2, keep.shape[1]
    place = first_column > 0
    del dense_in

    @pl.when(jnp.logical_not(in_middle()))
    def _():
        keep[...] = jnp.zeros_like(keep)
        send[...] = jnp.zeros_like(send)

    @pl.when(in_middle())
    def _():
        copy = fetch_codes((end_0, end_1, own_0, own_1, first, beside), staged, codes, sem)
        copy.start()
        total[...] = jnp.zeros_like(total)
        copy.wait()
        col, row = lax.axis_index("col"), lax.axis_index("row")
        if place:
            put_blocks(dense, first, codes, 4, 0, cut, slots, col)
            put_blocks(dense, second, codes, 4, cut, slots - cut, slots, col)
            put_blocks(dense, beside, codes, 5, cut, slots - cut, slots, col)
        next_row = jnp.where(row == 1, 0, 3)
        part = dense.at[:, pl.ds(first_column, columns)]
        multiply_group(part, total.at[0], (end_0, end_1), codes, 0, a_slots, next_row)
        multiply_group(part, total.at[1], (own_0, own_1), codes, 2, a_slots, row)
        for group in range(2):
            keep[pl.ds(group * rows, rows), :] = total[group, pl.ds(0, rows), :]
            send[pl.ds(group * rows, rows), :] = total[group, pl.ds(rows, rows), :]


def product(own, end, dense, late, first_column, columns, a_slots, slots):
    width = own[0].shape[1]
    half = jax.ShapeDtypeStruct((4 * width, columns), jnp.float32)
    return pl.pallas_call(
        functools.partial(product_body, a_slots, slots, first_column),
        out_shape=(jax.ShapeDtypeStruct(dense.shape, dense.dtype), half, half),
        in_specs=spaces(*"vvvvvvvv"),
        out_specs=tuple(spaces(*"vvv")),
        scratch_shapes=[pltpu.VMEM((2, 5 * width, columns), jnp.float32)] + code_scratch(),
        input_output_aliases={4: 0},
        compiler_params=pltpu.CompilerParams(vmem_limit_bytes=20 << 20),
    )(*own, *end, dense, *late)


def fold_body(keep, got, end_near, end_far, own_near, own_far):
    rows = end_near.shape[0]
    chip = lax.axis_index("layer") // 2
    extra = end_far.shape[0] - rows
    if extra:
        end_far[pl.ds(rows, extra), :] = jnp.zeros((extra, end_far.shape[1]), end_far.dtype)
    for first, near, far in ((0, end_near, end_far), (2 * rows, own_near, own_far)):
        for out, index in ((near, chip), (far, 1 - chip)):
            block = pl.ds(pl.multiple_of(first + index * rows, rows), rows)
            out[pl.ds(0, rows), :] = keep[block, :] + got[block, :]


def fold(keep, got, extra):
    rows, columns = keep.shape[0] // 4, keep.shape[1]
    part, longer = (jax.ShapeDtypeStruct((n, columns), jnp.float32) for n in (rows, rows + extra))
    return pl.pallas_call(
        fold_body,
        out_shape=(part, longer, part, part),
        in_specs=spaces(*"vv"),
        out_specs=tuple(spaces(*"vvvv")),
        compiler_params=pltpu.CompilerParams(vmem_limit_bytes=8 << 20),
    )(keep, got)


def settle_body(near, got, out):
    out[...] = (near[...] + got[...]).astype(out.dtype)


def settle(near, got):
    return pl.pallas_call(
        settle_body,
        out_shape=jax.ShapeDtypeStruct(near.shape, jnp.bfloat16),
        in_specs=spaces("v", "v"),
        out_specs=spaces("v")[0],
        compiler_params=pltpu.CompilerParams(vmem_limit_bytes=4 << 20),
    )(near, got)


def finish_body(left, left_got, right, right_got, near, far, settled, out):
    cut = left.shape[1]
    out[:, pl.ds(0, cut)] = ((left[...] + left_got[...]) + (near[...] + far[pl.ds(0, near.shape[0]), :])).astype(out.dtype)
    rest = (right[...] + right_got[...]) + settled[...].astype(jnp.float32)
    out[:, pl.ds(cut, rest.shape[1])] = rest.astype(out.dtype)


def finish(*parts):
    shape = (parts[0].shape[0], parts[0].shape[1] + parts[2].shape[1])
    return pl.pallas_call(
        finish_body,
        out_shape=jax.ShapeDtypeStruct(shape, jnp.bfloat16),
        in_specs=spaces(*"vvvvvvv"),
        out_specs=spaces("v")[0],
        compiler_params=pltpu.CompilerParams(vmem_limit_bytes=4 << 20),
    )(*parts)


BESIDE = [(0, 1), (1, 0), (2, 3), (3, 2)]
BEYOND = [(0, 2), (2, 3), (3, 1), (1, 0)]
COLS = [(0, 1), (1, 0)]
CORES = [(0, 1), (1, 0), (2, 3), (3, 2)]
EVERY = [(r, m) for r in range(4) for m in range(4)]
MIDDLE = [(r * 4 + m, (3 - r) * 4 + m if r in (1, 2) else r * 4 + (m ^ 1)) for r, m in EVERY]
CHIPS = [(r * 4 + m, r * 4 + (m ^ 2 if r in (1, 2) else m ^ 1)) for r, m in EVERY]
ACROSS = [(r * 4 + m, (r ^ 1) * 4 + (m ^ 2 if r in (1, 2) else m)) for r, m in EVERY]


def middle_shards(a_blocks, a_codes, b_blocks, b_codes):
    a_slots, slots = a_blocks.shape[0], b_blocks.shape[0]
    a_pack, b_pack, mixed, b_second = pack(a_codes, b_codes, a_blocks, b_blocks)
    b_across = lax.ppermute(b_pack, ("row", "layer"), MIDDLE)
    end_mixed = lax.ppermute(mixed, "row", BESIDE)
    far_second = lax.ppermute(b_second, "row", BEYOND)
    a_other = lax.ppermute(a_pack, "col", COLS)
    b_late, a_other = lax.optimization_barrier((b_second, a_other))
    end_second = lax.ppermute(b_late, "row", BESIDE)
    end_first, a_end = part(end_mixed, end_mixed.shape[0] - a_pack.shape[0])
    far_first = lax.ppermute(end_first, ("row", "layer"), MIDDLE)
    a_end, a_other = lax.optimization_barrier((a_end, a_other))
    a_end_other = lax.ppermute(a_end, "col", COLS)

    dense = early(b_pack, b_across, end_first, slots)
    columns = CB * a_blocks.shape[1]
    cut = columns * CUT // 4
    own, end = (a_pack, a_other), (a_end, a_end_other)
    late = (far_first, far_second, end_second)
    dense, keep, send = product(own, end, dense, late, cut, columns - cut, a_slots, slots)
    got = lax.ppermute(send, "layer", CORES)
    _, left_keep, left_send = product(own, end, dense, late, 0, cut, a_slots, slots)
    left_got = lax.ppermute(left_send, "layer", CORES)
    rest_near, rest_far, right, right_far = fold(keep, got, 0)
    rest_got = lax.ppermute(rest_far, ("row", "layer"), CHIPS)
    settled = lax.ppermute(settle(rest_near, rest_got), "row", BESIDE)
    right_got = lax.ppermute(right_far, ("row", "layer"), CHIPS)
    near, far, left, left_far = fold(left_keep, left_got, 8)
    got_near = lax.ppermute(near, "row", BESIDE)
    got_far = lax.ppermute(far, ("row", "layer"), ACROSS)
    left_got = lax.ppermute(left_far, ("row", "layer"), CHIPS)
    return finish(left, left_got, right, right_got, got_near, got_far, settled)


def solution(mesh):
    placed = (
        P(("row", "col", "layer"), None, None),
        P(("row", "col", "layer")),
        P(("row", "col", "layer"), None, None),
        P(("row", "col", "layer")),
    )
    body = middle_shards if middle_plan(mesh.shape) else shards
    return jax.shard_map(
        body, mesh=mesh, in_specs=placed, out_specs=P(("row", "layer"), "col"), check_vma=False
    )
```

```python
import functools

import jax
import jax.numpy as jnp
from jax import lax
from jax.experimental import pallas as pl
from jax.experimental.pallas import tpu as pltpu
from jax.sharding import PartitionSpec as P

RB = 4
CB = 4
KB = 6


def from_behind(block, axis, distance):
    devices = range(lax.axis_size(axis))
    route = [((i - distance) % len(devices), i) for i in devices]
    return lax.ppermute(block, axis, route)


def dense_left(block_stack, block_codes, part_index, pieces):
    block_width = block_stack.shape[1]
    is_live = block_codes >= 0
    row_of = block_codes // (pieces * KB)
    part_of = block_codes // KB % pieces
    inner_of = block_codes % KB
    selected = is_live & (part_of == part_index)
    row_hits = row_of[:, None] == jnp.arange(RB)[None, :]
    inner_hit = inner_of[:, None] == jnp.arange(KB)[None, :]
    weight = (selected[:, None, None] & row_hits[:, :, None] & inner_hit[:, None, :]).astype(
        jnp.bfloat16
    )
    dense_tile = jnp.einsum(
        "aik,axy->ixky", weight, block_stack, preferred_element_type=jnp.float32
    )
    return dense_tile.astype(jnp.bfloat16).reshape(RB * block_width, KB * block_width)


def dense_right(block_stack, block_codes):
    block_width = block_stack.shape[1]
    is_live = block_codes >= 0
    inner_of = block_codes // CB
    column_of = block_codes % CB
    inner_hit = inner_of[:, None] == jnp.arange(KB)[None, :]
    column_hit = column_of[:, None] == jnp.arange(CB)[None, :]
    weight = (is_live[:, None, None] & inner_hit[:, :, None] & column_hit[:, None, :]).astype(
        jnp.bfloat16
    )
    dense_tile = jnp.einsum(
        "skj,sxy->kxjy", weight, block_stack, preferred_element_type=jnp.float32
    )
    return dense_tile.astype(jnp.bfloat16).reshape(KB * block_width, CB * block_width)


def shards(a_blocks, a_codes, b_blocks, b_codes):
    row_count = lax.axis_size("row")
    col_count = lax.axis_size("col")
    pieces = row_count // col_count
    block_width = a_blocks.shape[1]
    row_index = lax.axis_index("row")
    col_index = lax.axis_index("col")
    a_stack, a_tags = (
        lax.all_to_all(a_blocks, "col", split_axis=0, concat_axis=0, tiled=True),
        lax.all_to_all(a_codes, "col", split_axis=0, concat_axis=0, tiled=True),
    )
    b_stack, b_tags = (
        lax.all_to_all(b_blocks, "row", split_axis=0, concat_axis=0, tiled=True),
        lax.all_to_all(b_codes, "row", split_axis=0, concat_axis=0, tiled=True),
    )

    def multiply(accumulated, left_stack, left_codes, right_stack, right_codes, piece_index):
        left_tile = dense_left(left_stack, left_codes, piece_index // col_count, pieces)
        right_tile = dense_right(right_stack, right_codes)
        return accumulated + jnp.dot(left_tile, right_tile, preferred_element_type=jnp.float32)

    start_sum = jnp.zeros((RB * block_width, CB * block_width), jnp.float32)

    def advance(visit_step, loop_state):
        accumulated, left_stack, left_codes, right_stack, right_codes = loop_state
        piece_index = (row_index + col_index + visit_step) % row_count
        accumulated = multiply(
            accumulated, left_stack, left_codes, right_stack, right_codes, piece_index
        )
        left_stack, left_codes = from_behind((left_stack, left_codes), "col", -1)
        right_stack, right_codes = from_behind((right_stack, right_codes), "row", -1)
        return (accumulated, left_stack, left_codes, right_stack, right_codes)

    loop_state = lax.fori_loop(
        0, row_count - 1, advance, (start_sum, a_stack, a_tags, b_stack, b_tags)
    )
    accumulated, left_stack, left_codes, right_stack, right_codes = loop_state
    last_piece = (row_index + col_index + row_count - 1) % row_count
    accumulated = multiply(
        accumulated, left_stack, left_codes, right_stack, right_codes, last_piece
    )
    reduced = lax.psum_scatter(accumulated, "layer", scatter_dimension=0, tiled=True)
    return reduced.astype(jnp.bfloat16)


CODE_ROWS = 16
FIRST = 8
CUT = 2


def middle_plan(mesh_shape):
    return (mesh_shape["row"], mesh_shape["col"], mesh_shape["layer"]) == (4, 2, 4)


def spaces(*names):
    kinds = {"s": pltpu.SMEM, "v": pltpu.VMEM, "h": pltpu.HBM}
    return [pl.BlockSpec(memory_space=kinds[name]) for name in names]


def first_slots(slots):
    return slots * FIRST // 16


def pack_body(a_tags, b_tags, a_ref, b_ref, a_out, b_out, mixed_out, second_out, a_codes, b_codes, sems):
    a_rows, b_rows = a_ref.shape[0], b_ref.shape[0]
    width = a_ref.shape[1]
    second = second_out.shape[0] - CODE_ROWS
    first = b_rows - second
    copies = [
        pltpu.make_async_copy(b_ref, b_out.at[pl.ds(0, b_rows)], sems.at[0]),
        pltpu.make_async_copy(a_ref, a_out.at[pl.ds(0, a_rows)], sems.at[1]),
        pltpu.make_async_copy(a_tags, a_codes, sems.at[2]),
        pltpu.make_async_copy(b_tags, b_codes, sems.at[3]),
    ]
    for copy in copies:
        copy.start()

    def code_rows(codes_ref):
        lanes = lax.broadcasted_iota(jnp.int32, (CODE_ROWS, width), 1)
        values = jnp.full((CODE_ROWS, width), -1, jnp.int32)
        for slot in range(codes_ref.shape[0]):
            values = jnp.where(lanes == slot, codes_ref[slot], values)
        return values.astype(jnp.float32).astype(jnp.bfloat16)

    copies[2].wait()
    copies[3].wait()
    a_tail, b_tail = code_rows(a_codes), code_rows(b_codes)
    a_out[pl.ds(a_rows, CODE_ROWS), :] = a_tail
    for index in range(3):
        b_out[pl.ds(b_rows + index * CODE_ROWS, CODE_ROWS), :] = b_tail
    mixed_out[pl.ds(first, CODE_ROWS), :] = b_tail
    mixed_out[pl.ds(first + CODE_ROWS + a_rows, CODE_ROWS), :] = a_tail
    second_out[pl.ds(second, CODE_ROWS), :] = b_tail
    copies[0].wait()
    mixed_out[pl.ds(0, first), :] = b_out[pl.ds(0, first), :]
    second_out[pl.ds(0, second), :] = b_out[pl.ds(first, second), :]
    copies[1].wait()
    mixed_out[pl.ds(first + CODE_ROWS, a_rows), :] = a_out[pl.ds(0, a_rows), :]


def pack(a_codes, b_codes, a_blocks, b_blocks):
    width = a_blocks.shape[1]
    a_flat = a_blocks.reshape(-1, width)
    b_flat = b_blocks.reshape(-1, width)
    a_rows, b_rows = a_flat.shape[0], b_flat.shape[0]
    first = first_slots(b_blocks.shape[0]) * width
    sizes = (
        a_rows + CODE_ROWS,
        b_rows + 3 * CODE_ROWS,
        first + a_rows + 2 * CODE_ROWS,
        b_rows - first + CODE_ROWS,
    )
    return pl.pallas_call(
        pack_body,
        out_shape=tuple(jax.ShapeDtypeStruct((rows, width), jnp.bfloat16) for rows in sizes),
        in_specs=spaces("h", "h", "h", "h"),
        out_specs=tuple(spaces("v", "v", "v", "v")),
        scratch_shapes=[
            pltpu.SMEM(a_codes.shape, jnp.int32),
            pltpu.SMEM(b_codes.shape, jnp.int32),
            pltpu.SemaphoreType.DMA((4,)),
        ],
        compiler_params=pltpu.CompilerParams(vmem_limit_bytes=8 << 20),
    )(*(pltpu.with_memory_space_constraint(x, pltpu.HBM) for x in (a_codes, b_codes, a_flat, b_flat)))


def part_body(mixed, first, second):
    rows = first.shape[0]
    first[...] = mixed[pl.ds(0, rows), :]
    second[...] = mixed[pl.ds(rows, second.shape[0]), :]


def part(mixed, rows):
    sizes = (rows, mixed.shape[0] - rows)
    return pl.pallas_call(
        part_body,
        out_shape=tuple(jax.ShapeDtypeStruct((n, mixed.shape[1]), mixed.dtype) for n in sizes),
        in_specs=spaces("v"),
        out_specs=tuple(spaces("v", "v")),
        compiler_params=pltpu.CompilerParams(vmem_limit_bytes=4 << 20),
    )(mixed)


def fetch_codes(packs, staged, codes, sem):
    for index, pack_ref in enumerate(packs):
        tail = pack_ref[pl.ds(pack_ref.shape[0] - CODE_ROWS, CODE_ROWS), :]
        staged[pl.ds(index, 1), :] = tail.astype(jnp.float32).astype(jnp.int32)[:1]
    return pltpu.make_async_copy(staged, codes, sem)


def code_scratch():
    return [
        pltpu.VMEM((8, 128), jnp.int32),
        pltpu.SMEM((8, 128), jnp.int32),
        pltpu.SemaphoreType.DMA(()),
    ]


def in_middle():
    row = lax.axis_index("row")
    return jnp.logical_or(row == 1, row == 2)


def put_blocks(dense, source, codes, line, first_slot, count, slots, col):
    width = source.shape[1]
    owners = 4
    for index in range(count):
        code = codes[line, first_slot + index]

        @pl.when(code >= 0)
        def _():
            piece = lax.rem((first_slot + index) // (slots // owners) + col, owners)
            inner = piece * KB + code // CB
            column = lax.rem(code, CB)
            dense[
                pl.ds(pl.multiple_of(inner * width, width), width),
                pl.ds(pl.multiple_of(column * width, width), width),
            ] = source[pl.ds(index * width, width), :]


def early_body(slots, own, across, first, dense, staged, codes, sem):
    cut = first_slots(slots)

    @pl.when(in_middle())
    def _():
        col = lax.axis_index("col")
        copy = fetch_codes((own, across, first), staged, codes, sem)
        copy.start()
        dense[...] = jnp.zeros_like(dense)
        copy.wait()
        put_blocks(dense, own, codes, 0, 0, slots, slots, col)
        put_blocks(dense, across, codes, 1, 0, slots, slots, col)
        put_blocks(dense, first, codes, 2, 0, cut, slots, col)


def early(own, across, first, slots):
    width = own.shape[1]
    return pl.pallas_call(
        functools.partial(early_body, slots),
        out_shape=jax.ShapeDtypeStruct((4 * KB * width, CB * width), jnp.bfloat16),
        in_specs=spaces("v", "v", "v"),
        out_specs=spaces("v")[0],
        scratch_shapes=code_scratch(),
        compiler_params=pltpu.CompilerParams(vmem_limit_bytes=12 << 20),
    )(own, across, first)


def more_body(slots, far, beside, dense_in, dense, staged, codes, sem):
    cut = first_slots(slots)
    del dense_in

    @pl.when(in_middle())
    def _():
        col = lax.axis_index("col")
        copy = fetch_codes((far, beside), staged, codes, sem)
        copy.start()
        copy.wait()
        put_blocks(dense, far, codes, 0, cut, slots - cut, slots, col)
        put_blocks(dense, beside, codes, 1, cut, slots - cut, slots, col)


def more(far, beside, dense, slots):
    return pl.pallas_call(
        functools.partial(more_body, slots),
        out_shape=jax.ShapeDtypeStruct(dense.shape, dense.dtype),
        in_specs=spaces("v", "v", "v"),
        out_specs=spaces("v")[0],
        scratch_shapes=code_scratch(),
        input_output_aliases={2: 0},
        compiler_params=pltpu.CompilerParams(vmem_limit_bytes=12 << 20),
    )(far, beside, dense)


def multiply_group(dense, total, packs, codes, line, slots, row):
    width = packs[0].shape[1]
    pieces, owners = 2, 2
    core = lax.rem(lax.axis_index("layer"), 2)
    for source in range(2):
        for slot in range(slots):
            code = codes[line + source, slot]
            live = (code >= 0).astype(jnp.int32)
            safe = jnp.maximum(code, 0)
            owner = slot // (slots // owners)
            piece = lax.rem(row + owner, owners) + owners * lax.rem(safe // KB, pieces)
            inner = piece * KB + lax.rem(safe, KB)
            block_row = safe // (pieces * KB)
            sent = (lax.rem(block_row, 2) != core).astype(jnp.int32)
            spot = live * (sent * 2 + block_row // 2) + (1 - live) * 4
            part = jnp.dot(
                packs[source][pl.ds(slot * width, width), :],
                dense[pl.ds(pl.multiple_of(inner * width, width), width), :],
                preferred_element_type=jnp.float32,
            )
            total[pl.ds(pl.multiple_of(spot * width, width), width), :] += part


def product_body(a_slots, slots, first_column, own_0, own_1, end_0, end_1, dense_in, first,
                 dense, keep, send, total, staged, codes, sem):
    cut = first_slots(slots)
    rows, columns = keep.shape[0] // 2, keep.shape[1]
    place = first_column > 0
    del dense_in

    @pl.when(jnp.logical_not(in_middle()))
    def _():
        keep[...] = jnp.zeros_like(keep)
        send[...] = jnp.zeros_like(send)

    @pl.when(in_middle())
    def _():
        copy = fetch_codes((end_0, end_1, own_0, own_1, first), staged, codes, sem)
        copy.start()
        total[...] = jnp.zeros_like(total)
        copy.wait()
        col, row = lax.axis_index("col"), lax.axis_index("row")
        if place:
            put_blocks(dense, first, codes, 4, 0, cut, slots, col)
        next_row = jnp.where(row == 1, 0, 3)
        part = dense.at[:, pl.ds(first_column, columns)]
        multiply_group(part, total.at[0], (end_0, end_1), codes, 0, a_slots, next_row)
        multiply_group(part, total.at[1], (own_0, own_1), codes, 2, a_slots, row)
        for group in range(2):
            keep[pl.ds(group * rows, rows), :] = total[group, pl.ds(0, rows), :]
            send[pl.ds(group * rows, rows), :] = total[group, pl.ds(rows, rows), :]


def product(own, end, dense, first, first_column, columns, a_slots, slots):
    width = own[0].shape[1]
    half = jax.ShapeDtypeStruct((4 * width, columns), jnp.float32)
    return pl.pallas_call(
        functools.partial(product_body, a_slots, slots, first_column),
        out_shape=(jax.ShapeDtypeStruct(dense.shape, dense.dtype), half, half),
        in_specs=spaces(*"vvvvvv"),
        out_specs=tuple(spaces(*"vvv")),
        scratch_shapes=[pltpu.VMEM((2, 5 * width, columns), jnp.float32)] + code_scratch(),
        input_output_aliases={4: 0},
        compiler_params=pltpu.CompilerParams(vmem_limit_bytes=20 << 20),
    )(*own, *end, dense, first)


def fold_body(keep, got, end_near, end_far, own_near, own_far):
    rows = end_near.shape[0]
    chip = lax.axis_index("layer") // 2
    extra = end_far.shape[0] - rows
    if extra:
        end_far[pl.ds(rows, extra), :] = jnp.zeros((extra, end_far.shape[1]), end_far.dtype)
    for first, near, far in ((0, end_near, end_far), (2 * rows, own_near, own_far)):
        for out, index in ((near, chip), (far, 1 - chip)):
            block = pl.ds(pl.multiple_of(first + index * rows, rows), rows)
            out[pl.ds(0, rows), :] = keep[block, :] + got[block, :]


def fold(keep, got, extra):
    rows, columns = keep.shape[0] // 4, keep.shape[1]
    part, longer = (jax.ShapeDtypeStruct((n, columns), jnp.float32) for n in (rows, rows + extra))
    return pl.pallas_call(
        fold_body,
        out_shape=(part, longer, part, part),
        in_specs=spaces(*"vv"),
        out_specs=tuple(spaces(*"vvvv")),
        compiler_params=pltpu.CompilerParams(vmem_limit_bytes=8 << 20),
    )(keep, got)


def settle_body(near, got, out):
    out[...] = (near[...] + got[...]).astype(out.dtype)


def settle(near, got):
    return pl.pallas_call(
        settle_body,
        out_shape=jax.ShapeDtypeStruct(near.shape, jnp.bfloat16),
        in_specs=spaces("v", "v"),
        out_specs=spaces("v")[0],
        compiler_params=pltpu.CompilerParams(vmem_limit_bytes=4 << 20),
    )(near, got)


def finish_body(left, left_got, right, right_got, near, far, settled, out):
    cut = left.shape[1]
    out[:, pl.ds(0, cut)] = ((left[...] + left_got[...]) + (near[...] + far[pl.ds(0, near.shape[0]), :])).astype(out.dtype)
    rest = (right[...] + right_got[...]) + settled[...].astype(jnp.float32)
    out[:, pl.ds(cut, rest.shape[1])] = rest.astype(out.dtype)


def finish(*parts):
    shape = (parts[0].shape[0], parts[0].shape[1] + parts[2].shape[1])
    return pl.pallas_call(
        finish_body,
        out_shape=jax.ShapeDtypeStruct(shape, jnp.bfloat16),
        in_specs=spaces(*"vvvvvvv"),
        out_specs=spaces("v")[0],
        compiler_params=pltpu.CompilerParams(vmem_limit_bytes=4 << 20),
    )(*parts)


BESIDE = [(0, 1), (1, 0), (2, 3), (3, 2)]
BEYOND = [(0, 2), (2, 3), (3, 1), (1, 0)]
COLS = [(0, 1), (1, 0)]
CORES = [(0, 1), (1, 0), (2, 3), (3, 2)]
EVERY = [(r, m) for r in range(4) for m in range(4)]
MIDDLE = [(r * 4 + m, (3 - r) * 4 + m if r in (1, 2) else r * 4 + (m ^ 1)) for r, m in EVERY]
CHIPS = [(r * 4 + m, r * 4 + (m ^ 2 if r in (1, 2) else m ^ 1)) for r, m in EVERY]
ACROSS = [(r * 4 + m, (r ^ 1) * 4 + (m ^ 2 if r in (1, 2) else m)) for r, m in EVERY]


def middle_shards(a_blocks, a_codes, b_blocks, b_codes):
    a_slots, slots = a_blocks.shape[0], b_blocks.shape[0]
    a_pack, b_pack, mixed, b_second = pack(a_codes, b_codes, a_blocks, b_blocks)
    b_across = lax.ppermute(b_pack, ("row", "layer"), MIDDLE)
    end_mixed = lax.ppermute(mixed, "row", BESIDE)
    far_second = lax.ppermute(b_second, "row", BEYOND)
    a_other = lax.ppermute(a_pack, "col", COLS)
    b_late, a_other = lax.optimization_barrier((b_second, a_other))
    end_second = lax.ppermute(b_late, "row", BESIDE)
    end_first, a_end = part(end_mixed, end_mixed.shape[0] - a_pack.shape[0])
    far_first = lax.ppermute(end_first, ("row", "layer"), MIDDLE)
    a_end, a_other = lax.optimization_barrier((a_end, a_other))
    a_end_other = lax.ppermute(a_end, "col", COLS)

    dense = early(b_pack, b_across, end_first, slots)
    columns = CB * a_blocks.shape[1]
    cut = columns * CUT // 4
    own, end = (a_pack, a_other), (a_end, a_end_other)
    dense = more(far_second, end_second, dense, slots)
    dense, keep, send = product(own, end, dense, far_first, cut, columns - cut, a_slots, slots)
    got = lax.ppermute(send, "layer", CORES)
    _, left_keep, left_send = product(own, end, dense, far_first, 0, cut, a_slots, slots)
    left_got = lax.ppermute(left_send, "layer", CORES)
    rest_near, rest_far, right, right_far = fold(keep, got, 0)
    rest_got = lax.ppermute(rest_far, ("row", "layer"), CHIPS)
    settled = lax.ppermute(settle(rest_near, rest_got), "row", BESIDE)
    right_got = lax.ppermute(right_far, ("row", "layer"), CHIPS)
    near, far, left, left_far = fold(left_keep, left_got, 8)
    got_near = lax.ppermute(near, "row", BESIDE)
    got_far = lax.ppermute(far, ("row", "layer"), ACROSS)
    left_got = lax.ppermute(left_far, ("row", "layer"), CHIPS)
    return finish(left, left_got, right, right_got, got_near, got_far, settled)


def solution(mesh):
    placed = (
        P(("row", "col", "layer"), None, None),
        P(("row", "col", "layer")),
        P(("row", "col", "layer"), None, None),
        P(("row", "col", "layer")),
    )
    body = middle_shards if middle_plan(mesh.shape) else shards
    return jax.shard_map(
        body, mesh=mesh, in_specs=placed, out_specs=P(("row", "layer"), "col"), check_vma=False
    )
```

```python
import functools

import jax
import jax.numpy as jnp
from jax import lax
from jax.experimental import pallas as pl
from jax.experimental.pallas import tpu as pltpu
from jax.sharding import PartitionSpec as P

RB = 4
CB = 4
KB = 6


def from_behind(block, axis, distance):
    devices = range(lax.axis_size(axis))
    route = [((i - distance) % len(devices), i) for i in devices]
    return lax.ppermute(block, axis, route)


def dense_left(block_stack, block_codes, part_index, pieces):
    block_width = block_stack.shape[1]
    is_live = block_codes >= 0
    row_of = block_codes // (pieces * KB)
    part_of = block_codes // KB % pieces
    inner_of = block_codes % KB
    selected = is_live & (part_of == part_index)
    row_hits = row_of[:, None] == jnp.arange(RB)[None, :]
    inner_hit = inner_of[:, None] == jnp.arange(KB)[None, :]
    weight = (selected[:, None, None] & row_hits[:, :, None] & inner_hit[:, None, :]).astype(
        jnp.bfloat16
    )
    dense_tile = jnp.einsum(
        "aik,axy->ixky", weight, block_stack, preferred_element_type=jnp.float32
    )
    return dense_tile.astype(jnp.bfloat16).reshape(RB * block_width, KB * block_width)


def dense_right(block_stack, block_codes):
    block_width = block_stack.shape[1]
    is_live = block_codes >= 0
    inner_of = block_codes // CB
    column_of = block_codes % CB
    inner_hit = inner_of[:, None] == jnp.arange(KB)[None, :]
    column_hit = column_of[:, None] == jnp.arange(CB)[None, :]
    weight = (is_live[:, None, None] & inner_hit[:, :, None] & column_hit[:, None, :]).astype(
        jnp.bfloat16
    )
    dense_tile = jnp.einsum(
        "skj,sxy->kxjy", weight, block_stack, preferred_element_type=jnp.float32
    )
    return dense_tile.astype(jnp.bfloat16).reshape(KB * block_width, CB * block_width)


def shards(a_blocks, a_codes, b_blocks, b_codes):
    row_count = lax.axis_size("row")
    col_count = lax.axis_size("col")
    pieces = row_count // col_count
    block_width = a_blocks.shape[1]
    row_index = lax.axis_index("row")
    col_index = lax.axis_index("col")
    a_stack, a_tags = (
        lax.all_to_all(a_blocks, "col", split_axis=0, concat_axis=0, tiled=True),
        lax.all_to_all(a_codes, "col", split_axis=0, concat_axis=0, tiled=True),
    )
    b_stack, b_tags = (
        lax.all_to_all(b_blocks, "row", split_axis=0, concat_axis=0, tiled=True),
        lax.all_to_all(b_codes, "row", split_axis=0, concat_axis=0, tiled=True),
    )

    def multiply(accumulated, left_stack, left_codes, right_stack, right_codes, piece_index):
        left_tile = dense_left(left_stack, left_codes, piece_index // col_count, pieces)
        right_tile = dense_right(right_stack, right_codes)
        return accumulated + jnp.dot(left_tile, right_tile, preferred_element_type=jnp.float32)

    start_sum = jnp.zeros((RB * block_width, CB * block_width), jnp.float32)

    def advance(visit_step, loop_state):
        accumulated, left_stack, left_codes, right_stack, right_codes = loop_state
        piece_index = (row_index + col_index + visit_step) % row_count
        accumulated = multiply(
            accumulated, left_stack, left_codes, right_stack, right_codes, piece_index
        )
        left_stack, left_codes = from_behind((left_stack, left_codes), "col", -1)
        right_stack, right_codes = from_behind((right_stack, right_codes), "row", -1)
        return (accumulated, left_stack, left_codes, right_stack, right_codes)

    loop_state = lax.fori_loop(
        0, row_count - 1, advance, (start_sum, a_stack, a_tags, b_stack, b_tags)
    )
    accumulated, left_stack, left_codes, right_stack, right_codes = loop_state
    last_piece = (row_index + col_index + row_count - 1) % row_count
    accumulated = multiply(
        accumulated, left_stack, left_codes, right_stack, right_codes, last_piece
    )
    reduced = lax.psum_scatter(accumulated, "layer", scatter_dimension=0, tiled=True)
    return reduced.astype(jnp.bfloat16)


CODE_ROWS = 16
FIRST = 8
CUT = 2


def middle_plan(mesh_shape):
    return (mesh_shape["row"], mesh_shape["col"], mesh_shape["layer"]) == (4, 2, 4)


def spaces(*names):
    kinds = {"s": pltpu.SMEM, "v": pltpu.VMEM, "h": pltpu.HBM}
    return [pl.BlockSpec(memory_space=kinds[name]) for name in names]


def first_slots(slots):
    return slots * FIRST // 16


def pack_body(a_tags, b_tags, a_ref, b_ref, a_out, b_out, mixed_out, second_out, a_codes, b_codes, sems):
    a_rows, b_rows = a_ref.shape[0], b_ref.shape[0]
    width = a_ref.shape[1]
    second = second_out.shape[0] - CODE_ROWS
    first = b_rows - second
    copies = [
        pltpu.make_async_copy(b_ref, b_out.at[pl.ds(0, b_rows)], sems.at[0]),
        pltpu.make_async_copy(a_ref, a_out.at[pl.ds(0, a_rows)], sems.at[1]),
        pltpu.make_async_copy(a_tags, a_codes, sems.at[2]),
        pltpu.make_async_copy(b_tags, b_codes, sems.at[3]),
    ]
    for copy in copies:
        copy.start()

    def code_rows(codes_ref):
        lanes = lax.broadcasted_iota(jnp.int32, (CODE_ROWS, width), 1)
        values = jnp.full((CODE_ROWS, width), -1, jnp.int32)
        for slot in range(codes_ref.shape[0]):
            values = jnp.where(lanes == slot, codes_ref[slot], values)
        return values.astype(jnp.float32).astype(jnp.bfloat16)

    copies[2].wait()
    copies[3].wait()
    a_tail, b_tail = code_rows(a_codes), code_rows(b_codes)
    a_out[pl.ds(a_rows, CODE_ROWS), :] = a_tail
    for index in range(3):
        b_out[pl.ds(b_rows + index * CODE_ROWS, CODE_ROWS), :] = b_tail
    mixed_out[pl.ds(first, CODE_ROWS), :] = b_tail
    mixed_out[pl.ds(first + CODE_ROWS + a_rows, CODE_ROWS), :] = a_tail
    second_out[pl.ds(second, CODE_ROWS), :] = b_tail
    copies[0].wait()
    mixed_out[pl.ds(0, first), :] = b_out[pl.ds(0, first), :]
    second_out[pl.ds(0, second), :] = b_out[pl.ds(first, second), :]
    copies[1].wait()
    mixed_out[pl.ds(first + CODE_ROWS, a_rows), :] = a_out[pl.ds(0, a_rows), :]


def pack(a_codes, b_codes, a_blocks, b_blocks):
    width = a_blocks.shape[1]
    a_flat = a_blocks.reshape(-1, width)
    b_flat = b_blocks.reshape(-1, width)
    a_rows, b_rows = a_flat.shape[0], b_flat.shape[0]
    first = first_slots(b_blocks.shape[0]) * width
    sizes = (
        a_rows + CODE_ROWS,
        b_rows + 3 * CODE_ROWS,
        first + a_rows + 2 * CODE_ROWS,
        b_rows - first + CODE_ROWS,
    )
    return pl.pallas_call(
        pack_body,
        out_shape=tuple(jax.ShapeDtypeStruct((rows, width), jnp.bfloat16) for rows in sizes),
        in_specs=spaces("h", "h", "h", "h"),
        out_specs=tuple(spaces("v", "v", "v", "v")),
        scratch_shapes=[
            pltpu.SMEM(a_codes.shape, jnp.int32),
            pltpu.SMEM(b_codes.shape, jnp.int32),
            pltpu.SemaphoreType.DMA((4,)),
        ],
        compiler_params=pltpu.CompilerParams(vmem_limit_bytes=8 << 20),
    )(*(pltpu.with_memory_space_constraint(x, pltpu.HBM) for x in (a_codes, b_codes, a_flat, b_flat)))


def part_body(mixed, first, second):
    rows = first.shape[0]
    first[...] = mixed[pl.ds(0, rows), :]
    second[...] = mixed[pl.ds(rows, second.shape[0]), :]


def part(mixed, rows):
    sizes = (rows, mixed.shape[0] - rows)
    return pl.pallas_call(
        part_body,
        out_shape=tuple(jax.ShapeDtypeStruct((n, mixed.shape[1]), mixed.dtype) for n in sizes),
        in_specs=spaces("v"),
        out_specs=tuple(spaces("v", "v")),
        compiler_params=pltpu.CompilerParams(vmem_limit_bytes=4 << 20),
    )(mixed)


def fetch_codes(packs, staged, codes, sem):
    for index, pack_ref in enumerate(packs):
        tail = pack_ref[pl.ds(pack_ref.shape[0] - CODE_ROWS, CODE_ROWS), :]
        staged[pl.ds(index, 1), :] = tail.astype(jnp.float32).astype(jnp.int32)[:1]
    return pltpu.make_async_copy(staged, codes, sem)


def code_scratch():
    return [
        pltpu.VMEM((8, 128), jnp.int32),
        pltpu.SMEM((8, 128), jnp.int32),
        pltpu.SemaphoreType.DMA(()),
    ]


def in_middle():
    row = lax.axis_index("row")
    return jnp.logical_or(row == 1, row == 2)


def put_blocks(dense, source, codes, line, first_slot, count, slots, col):
    width = source.shape[1]
    owners = 4
    for index in range(count):
        code = codes[line, first_slot + index]

        @pl.when(code >= 0)
        def _():
            piece = lax.rem((first_slot + index) // (slots // owners) + col, owners)
            inner = piece * KB + code // CB
            column = lax.rem(code, CB)
            dense[
                pl.ds(pl.multiple_of(inner * width, width), width),
                pl.ds(pl.multiple_of(column * width, width), width),
            ] = source[pl.ds(index * width, width), :]


def early_body(slots, own, across, first, dense, staged, codes, sem):
    cut = first_slots(slots)

    @pl.when(in_middle())
    def _():
        col = lax.axis_index("col")
        copy = fetch_codes((own, across, first), staged, codes, sem)
        copy.start()
        dense[...] = jnp.zeros_like(dense)
        copy.wait()
        put_blocks(dense, own, codes, 0, 0, slots, slots, col)
        put_blocks(dense, across, codes, 1, 0, slots, slots, col)
        put_blocks(dense, first, codes, 2, 0, cut, slots, col)


def early(own, across, first, slots):
    width = own.shape[1]
    return pl.pallas_call(
        functools.partial(early_body, slots),
        out_shape=jax.ShapeDtypeStruct((4 * KB * width, CB * width), jnp.bfloat16),
        in_specs=spaces("v", "v", "v"),
        out_specs=spaces("v")[0],
        scratch_shapes=code_scratch(),
        compiler_params=pltpu.CompilerParams(vmem_limit_bytes=12 << 20),
    )(own, across, first)


def more_body(slots, far, beside, dense_in, dense, staged, codes, sem):
    cut = first_slots(slots)
    del dense_in

    @pl.when(in_middle())
    def _():
        col = lax.axis_index("col")
        copy = fetch_codes((far, beside), staged, codes, sem)
        copy.start()
        copy.wait()
        put_blocks(dense, far, codes, 0, cut, slots - cut, slots, col)
        put_blocks(dense, beside, codes, 1, cut, slots - cut, slots, col)


def more(far, beside, dense, slots):
    return pl.pallas_call(
        functools.partial(more_body, slots),
        out_shape=jax.ShapeDtypeStruct(dense.shape, dense.dtype),
        in_specs=spaces("v", "v", "v"),
        out_specs=spaces("v")[0],
        scratch_shapes=code_scratch(),
        input_output_aliases={2: 0},
        compiler_params=pltpu.CompilerParams(vmem_limit_bytes=12 << 20),
    )(far, beside, dense)


def multiply_groups(dense, totals, groups, codes, slots, rows):
    width = groups[0][0].shape[1]
    pieces, owners = 2, 2
    core = lax.rem(lax.axis_index("layer"), 2)
    for source in range(2):
        for slot in range(slots):
            for group, (total, packs, row) in enumerate(zip(totals, groups, rows)):
                code = codes[2 * group + source, slot]
                live = (code >= 0).astype(jnp.int32)
                safe = jnp.maximum(code, 0)
                owner = slot // (slots // owners)
                piece = lax.rem(row + owner, owners) + owners * lax.rem(safe // KB, pieces)
                inner = piece * KB + lax.rem(safe, KB)
                block_row = safe // (pieces * KB)
                sent = (lax.rem(block_row, 2) != core).astype(jnp.int32)
                spot = live * (sent * 2 + block_row // 2) + (1 - live) * 4
                part = jnp.dot(
                    packs[source][pl.ds(slot * width, width), :],
                    dense[pl.ds(pl.multiple_of(inner * width, width), width), :],
                    preferred_element_type=jnp.float32,
                )
                total[pl.ds(pl.multiple_of(spot * width, width), width), :] += part


def product_body(a_slots, slots, first_column, own_0, own_1, end_0, end_1, dense_in, first,
                 dense, keep, send, end_total, own_total, staged, codes, sem):
    cut = first_slots(slots)
    rows, columns = keep.shape[0] // 2, keep.shape[1]
    place = first_column > 0
    del dense_in

    @pl.when(jnp.logical_not(in_middle()))
    def _():
        keep[...] = jnp.zeros_like(keep)
        send[...] = jnp.zeros_like(send)

    @pl.when(in_middle())
    def _():
        copy = fetch_codes((end_0, end_1, own_0, own_1, first), staged, codes, sem)
        copy.start()
        for total in (end_total, own_total):
            total[pl.ds(0, 2 * rows), :] = jnp.zeros((2 * rows, columns), total.dtype)
        copy.wait()
        col, row = lax.axis_index("col"), lax.axis_index("row")
        if place:
            put_blocks(dense, first, codes, 4, 0, cut, slots, col)
        next_row = jnp.where(row == 1, 0, 3)
        part = dense.at[:, pl.ds(first_column, columns)]
        multiply_groups(part, (end_total, own_total), ((end_0, end_1), (own_0, own_1)), codes, a_slots, (next_row, row))
        for group, total in enumerate((end_total, own_total)):
            keep[pl.ds(group * rows, rows), :] = total[pl.ds(0, rows), :]
            send[pl.ds(group * rows, rows), :] = total[pl.ds(rows, rows), :]


def product(own, end, dense, first, first_column, columns, a_slots, slots):
    width = own[0].shape[1]
    half = jax.ShapeDtypeStruct((4 * width, columns), jnp.float32)
    return pl.pallas_call(
        functools.partial(product_body, a_slots, slots, first_column),
        out_shape=(jax.ShapeDtypeStruct(dense.shape, dense.dtype), half, half),
        in_specs=spaces(*"vvvvvv"),
        out_specs=tuple(spaces(*"vvv")),
        scratch_shapes=[pltpu.VMEM((5 * width, columns), jnp.float32)] * 2 + code_scratch(),
        input_output_aliases={4: 0},
        compiler_params=pltpu.CompilerParams(vmem_limit_bytes=20 << 20),
    )(*own, *end, dense, first)


def fold_body(keep, got, end_near, end_far, own_near, own_far):
    rows = end_near.shape[0]
    chip = lax.axis_index("layer") // 2
    extra = end_far.shape[0] - rows
    if extra:
        end_far[pl.ds(rows, extra), :] = jnp.zeros((extra, end_far.shape[1]), end_far.dtype)
    for first, near, far in ((0, end_near, end_far), (2 * rows, own_near, own_far)):
        for out, index in ((near, chip), (far, 1 - chip)):
            block = pl.ds(pl.multiple_of(first + index * rows, rows), rows)
            out[pl.ds(0, rows), :] = keep[block, :] + got[block, :]


def fold(keep, got, extra):
    rows, columns = keep.shape[0] // 4, keep.shape[1]
    part, longer = (jax.ShapeDtypeStruct((n, columns), jnp.float32) for n in (rows, rows + extra))
    return pl.pallas_call(
        fold_body,
        out_shape=(part, longer, part, part),
        in_specs=spaces(*"vv"),
        out_specs=tuple(spaces(*"vvvv")),
        compiler_params=pltpu.CompilerParams(vmem_limit_bytes=8 << 20),
    )(keep, got)


def settle_body(near, got, out):
    out[...] = (near[...] + got[...]).astype(out.dtype)


def settle(near, got):
    return pl.pallas_call(
        settle_body,
        out_shape=jax.ShapeDtypeStruct(near.shape, jnp.bfloat16),
        in_specs=spaces("v", "v"),
        out_specs=spaces("v")[0],
        compiler_params=pltpu.CompilerParams(vmem_limit_bytes=4 << 20),
    )(near, got)


def finish_body(left, left_got, right, right_got, near, far, settled, out):
    cut = left.shape[1]
    out[:, pl.ds(0, cut)] = ((left[...] + left_got[...]) + (near[...] + far[pl.ds(0, near.shape[0]), :])).astype(out.dtype)
    rest = (right[...] + right_got[...]) + settled[...].astype(jnp.float32)
    out[:, pl.ds(cut, rest.shape[1])] = rest.astype(out.dtype)


def finish(*parts):
    shape = (parts[0].shape[0], parts[0].shape[1] + parts[2].shape[1])
    return pl.pallas_call(
        finish_body,
        out_shape=jax.ShapeDtypeStruct(shape, jnp.bfloat16),
        in_specs=spaces(*"vvvvvvv"),
        out_specs=spaces("v")[0],
        compiler_params=pltpu.CompilerParams(vmem_limit_bytes=4 << 20),
    )(*parts)


BESIDE = [(0, 1), (1, 0), (2, 3), (3, 2)]
BEYOND = [(0, 2), (2, 3), (3, 1), (1, 0)]
COLS = [(0, 1), (1, 0)]
CORES = [(0, 1), (1, 0), (2, 3), (3, 2)]
EVERY = [(r, m) for r in range(4) for m in range(4)]
MIDDLE = [(r * 4 + m, (3 - r) * 4 + m if r in (1, 2) else r * 4 + (m ^ 1)) for r, m in EVERY]
CHIPS = [(r * 4 + m, r * 4 + (m ^ 2 if r in (1, 2) else m ^ 1)) for r, m in EVERY]
ACROSS = [(r * 4 + m, (r ^ 1) * 4 + (m ^ 2 if r in (1, 2) else m)) for r, m in EVERY]


def middle_shards(a_blocks, a_codes, b_blocks, b_codes):
    a_slots, slots = a_blocks.shape[0], b_blocks.shape[0]
    a_pack, b_pack, mixed, b_second = pack(a_codes, b_codes, a_blocks, b_blocks)
    b_across = lax.ppermute(b_pack, ("row", "layer"), MIDDLE)
    end_mixed = lax.ppermute(mixed, "row", BESIDE)
    far_second = lax.ppermute(b_second, "row", BEYOND)
    a_other = lax.ppermute(a_pack, "col", COLS)
    b_late, a_other = lax.optimization_barrier((b_second, a_other))
    end_second = lax.ppermute(b_late, "row", BESIDE)
    end_first, a_end = part(end_mixed, end_mixed.shape[0] - a_pack.shape[0])
    far_first = lax.ppermute(end_first, ("row", "layer"), MIDDLE)
    a_end, a_other = lax.optimization_barrier((a_end, a_other))
    a_end_other = lax.ppermute(a_end, "col", COLS)

    dense = early(b_pack, b_across, end_first, slots)
    columns = CB * a_blocks.shape[1]
    cut = columns * CUT // 4
    own, end = (a_pack, a_other), (a_end, a_end_other)
    dense = more(far_second, end_second, dense, slots)
    dense, keep, send = product(own, end, dense, far_first, cut, columns - cut, a_slots, slots)
    got = lax.ppermute(send, "layer", CORES)
    _, left_keep, left_send = product(own, end, dense, far_first, 0, cut, a_slots, slots)
    left_got = lax.ppermute(left_send, "layer", CORES)
    rest_near, rest_far, right, right_far = fold(keep, got, 0)
    rest_got = lax.ppermute(rest_far, ("row", "layer"), CHIPS)
    settled = lax.ppermute(settle(rest_near, rest_got), "row", BESIDE)
    right_got = lax.ppermute(right_far, ("row", "layer"), CHIPS)
    near, far, left, left_far = fold(left_keep, left_got, 8)
    got_near = lax.ppermute(near, "row", BESIDE)
    got_far = lax.ppermute(far, ("row", "layer"), ACROSS)
    left_got = lax.ppermute(left_far, ("row", "layer"), CHIPS)
    return finish(left, left_got, right, right_got, got_near, got_far, settled)


def solution(mesh):
    placed = (
        P(("row", "col", "layer"), None, None),
        P(("row", "col", "layer")),
        P(("row", "col", "layer"), None, None),
        P(("row", "col", "layer")),
    )
    body = middle_shards if middle_plan(mesh.shape) else shards
    return jax.shard_map(
        body, mesh=mesh, in_specs=placed, out_specs=P(("row", "layer"), "col"), check_vma=False
    )
```

```python
import functools

import jax
import jax.numpy as jnp
from jax import lax
from jax.experimental import pallas as pl
from jax.experimental.pallas import tpu as pltpu
from jax.sharding import PartitionSpec as P

RB = 4
CB = 4
KB = 6


def from_behind(block, axis, distance):
    devices = range(lax.axis_size(axis))
    route = [((i - distance) % len(devices), i) for i in devices]
    return lax.ppermute(block, axis, route)


def dense_left(block_stack, block_codes, part_index, pieces):
    block_width = block_stack.shape[1]
    is_live = block_codes >= 0
    row_of = block_codes // (pieces * KB)
    part_of = block_codes // KB % pieces
    inner_of = block_codes % KB
    selected = is_live & (part_of == part_index)
    row_hits = row_of[:, None] == jnp.arange(RB)[None, :]
    inner_hit = inner_of[:, None] == jnp.arange(KB)[None, :]
    weight = (selected[:, None, None] & row_hits[:, :, None] & inner_hit[:, None, :]).astype(
        jnp.bfloat16
    )
    dense_tile = jnp.einsum(
        "aik,axy->ixky", weight, block_stack, preferred_element_type=jnp.float32
    )
    return dense_tile.astype(jnp.bfloat16).reshape(RB * block_width, KB * block_width)


def dense_right(block_stack, block_codes):
    block_width = block_stack.shape[1]
    is_live = block_codes >= 0
    inner_of = block_codes // CB
    column_of = block_codes % CB
    inner_hit = inner_of[:, None] == jnp.arange(KB)[None, :]
    column_hit = column_of[:, None] == jnp.arange(CB)[None, :]
    weight = (is_live[:, None, None] & inner_hit[:, :, None] & column_hit[:, None, :]).astype(
        jnp.bfloat16
    )
    dense_tile = jnp.einsum(
        "skj,sxy->kxjy", weight, block_stack, preferred_element_type=jnp.float32
    )
    return dense_tile.astype(jnp.bfloat16).reshape(KB * block_width, CB * block_width)


def shards(a_blocks, a_codes, b_blocks, b_codes):
    row_count = lax.axis_size("row")
    col_count = lax.axis_size("col")
    pieces = row_count // col_count
    block_width = a_blocks.shape[1]
    row_index = lax.axis_index("row")
    col_index = lax.axis_index("col")
    a_stack, a_tags = (
        lax.all_to_all(a_blocks, "col", split_axis=0, concat_axis=0, tiled=True),
        lax.all_to_all(a_codes, "col", split_axis=0, concat_axis=0, tiled=True),
    )
    b_stack, b_tags = (
        lax.all_to_all(b_blocks, "row", split_axis=0, concat_axis=0, tiled=True),
        lax.all_to_all(b_codes, "row", split_axis=0, concat_axis=0, tiled=True),
    )

    def multiply(accumulated, left_stack, left_codes, right_stack, right_codes, piece_index):
        left_tile = dense_left(left_stack, left_codes, piece_index // col_count, pieces)
        right_tile = dense_right(right_stack, right_codes)
        return accumulated + jnp.dot(left_tile, right_tile, preferred_element_type=jnp.float32)

    start_sum = jnp.zeros((RB * block_width, CB * block_width), jnp.float32)

    def advance(visit_step, loop_state):
        accumulated, left_stack, left_codes, right_stack, right_codes = loop_state
        piece_index = (row_index + col_index + visit_step) % row_count
        accumulated = multiply(
            accumulated, left_stack, left_codes, right_stack, right_codes, piece_index
        )
        left_stack, left_codes = from_behind((left_stack, left_codes), "col", -1)
        right_stack, right_codes = from_behind((right_stack, right_codes), "row", -1)
        return (accumulated, left_stack, left_codes, right_stack, right_codes)

    loop_state = lax.fori_loop(
        0, row_count - 1, advance, (start_sum, a_stack, a_tags, b_stack, b_tags)
    )
    accumulated, left_stack, left_codes, right_stack, right_codes = loop_state
    last_piece = (row_index + col_index + row_count - 1) % row_count
    accumulated = multiply(
        accumulated, left_stack, left_codes, right_stack, right_codes, last_piece
    )
    reduced = lax.psum_scatter(accumulated, "layer", scatter_dimension=0, tiled=True)
    return reduced.astype(jnp.bfloat16)


CODE_ROWS = 16
FIRST = 8
CUT = 2


def middle_plan(mesh_shape):
    return (mesh_shape["row"], mesh_shape["col"], mesh_shape["layer"]) == (4, 2, 4)


def spaces(*names):
    kinds = {"s": pltpu.SMEM, "v": pltpu.VMEM, "h": pltpu.HBM}
    return [pl.BlockSpec(memory_space=kinds[name]) for name in names]


def first_slots(slots):
    return slots * FIRST // 16


def pack_body(a_tags, b_tags, a_ref, b_ref, a_out, b_out, mixed_out, second_out, a_codes, b_codes, sems):
    a_rows, b_rows = a_ref.shape[0], b_ref.shape[0]
    width = a_ref.shape[1]
    second = second_out.shape[0] - CODE_ROWS
    first = b_rows - second
    copies = [
        pltpu.make_async_copy(b_ref, b_out.at[pl.ds(0, b_rows)], sems.at[0]),
        pltpu.make_async_copy(a_ref, a_out.at[pl.ds(0, a_rows)], sems.at[1]),
        pltpu.make_async_copy(a_tags, a_codes, sems.at[2]),
        pltpu.make_async_copy(b_tags, b_codes, sems.at[3]),
    ]
    for copy in copies:
        copy.start()

    def code_rows(codes_ref):
        lanes = lax.broadcasted_iota(jnp.int32, (CODE_ROWS, width), 1)
        values = jnp.full((CODE_ROWS, width), -1, jnp.int32)
        for slot in range(codes_ref.shape[0]):
            values = jnp.where(lanes == slot, codes_ref[slot], values)
        return values.astype(jnp.float32).astype(jnp.bfloat16)

    copies[2].wait()
    copies[3].wait()
    a_tail, b_tail = code_rows(a_codes), code_rows(b_codes)
    a_out[pl.ds(a_rows, CODE_ROWS), :] = a_tail
    for index in range(3):
        b_out[pl.ds(b_rows + index * CODE_ROWS, CODE_ROWS), :] = b_tail
    mixed_out[pl.ds(first, CODE_ROWS), :] = b_tail
    mixed_out[pl.ds(first + CODE_ROWS + a_rows, CODE_ROWS), :] = a_tail
    second_out[pl.ds(second, CODE_ROWS), :] = b_tail
    copies[0].wait()
    mixed_out[pl.ds(0, first), :] = b_out[pl.ds(0, first), :]
    second_out[pl.ds(0, second), :] = b_out[pl.ds(first, second), :]
    copies[1].wait()
    mixed_out[pl.ds(first + CODE_ROWS, a_rows), :] = a_out[pl.ds(0, a_rows), :]


def pack(a_codes, b_codes, a_blocks, b_blocks):
    width = a_blocks.shape[1]
    a_flat = a_blocks.reshape(-1, width)
    b_flat = b_blocks.reshape(-1, width)
    a_rows, b_rows = a_flat.shape[0], b_flat.shape[0]
    first = first_slots(b_blocks.shape[0]) * width
    sizes = (
        a_rows + CODE_ROWS,
        b_rows + 3 * CODE_ROWS,
        first + a_rows + 2 * CODE_ROWS,
        b_rows - first + CODE_ROWS,
    )
    return pl.pallas_call(
        pack_body,
        out_shape=tuple(jax.ShapeDtypeStruct((rows, width), jnp.bfloat16) for rows in sizes),
        in_specs=spaces("h", "h", "h", "h"),
        out_specs=tuple(spaces("v", "v", "v", "v")),
        scratch_shapes=[
            pltpu.SMEM(a_codes.shape, jnp.int32),
            pltpu.SMEM(b_codes.shape, jnp.int32),
            pltpu.SemaphoreType.DMA((4,)),
        ],
        compiler_params=pltpu.CompilerParams(vmem_limit_bytes=8 << 20),
    )(*(pltpu.with_memory_space_constraint(x, pltpu.HBM) for x in (a_codes, b_codes, a_flat, b_flat)))


def part_body(mixed, first, second):
    rows = first.shape[0]
    first[...] = mixed[pl.ds(0, rows), :]
    second[...] = mixed[pl.ds(rows, second.shape[0]), :]


def part(mixed, rows):
    sizes = (rows, mixed.shape[0] - rows)
    return pl.pallas_call(
        part_body,
        out_shape=tuple(jax.ShapeDtypeStruct((n, mixed.shape[1]), mixed.dtype) for n in sizes),
        in_specs=spaces("v"),
        out_specs=tuple(spaces("v", "v")),
        compiler_params=pltpu.CompilerParams(vmem_limit_bytes=4 << 20),
    )(mixed)


def fetch_codes(packs, staged, codes, sem):
    for index, pack_ref in enumerate(packs):
        tail = pack_ref[pl.ds(pack_ref.shape[0] - CODE_ROWS, CODE_ROWS), :]
        staged[pl.ds(index, 1), :] = tail.astype(jnp.float32).astype(jnp.int32)[:1]
    return pltpu.make_async_copy(staged, codes, sem)


def code_scratch():
    return [
        pltpu.VMEM((8, 128), jnp.int32),
        pltpu.SMEM((8, 128), jnp.int32),
        pltpu.SemaphoreType.DMA(()),
    ]


def in_middle():
    row = lax.axis_index("row")
    return jnp.logical_or(row == 1, row == 2)


def put_blocks(dense, source, codes, line, first_slot, count, slots, col):
    width = source.shape[1]
    owners = 4
    for index in range(count):
        code = codes[line, first_slot + index]
        piece = lax.rem((first_slot + index) // (slots // owners) + col, owners)
        inner = jnp.where(code >= 0, piece * KB + code // CB, dense.shape[0] // width - 1)
        column = lax.rem(jnp.maximum(code, 0), CB)
        dense[
            pl.ds(pl.multiple_of(inner * width, width), width),
            pl.ds(pl.multiple_of(column * width, width), width),
        ] = source[pl.ds(index * width, width), :]


def early_body(slots, own, across, first, dense, staged, codes, sem):
    cut = first_slots(slots)

    @pl.when(in_middle())
    def _():
        col = lax.axis_index("col")
        copy = fetch_codes((own, across, first), staged, codes, sem)
        copy.start()
        dense[...] = jnp.zeros_like(dense)
        copy.wait()
        put_blocks(dense, own, codes, 0, 0, slots, slots, col)
        put_blocks(dense, across, codes, 1, 0, slots, slots, col)
        put_blocks(dense, first, codes, 2, 0, cut, slots, col)


def early(own, across, first, slots):
    width = own.shape[1]
    return pl.pallas_call(
        functools.partial(early_body, slots),
        out_shape=jax.ShapeDtypeStruct(((4 * KB + 1) * width, CB * width), jnp.bfloat16),
        in_specs=spaces("v", "v", "v"),
        out_specs=spaces("v")[0],
        scratch_shapes=code_scratch(),
        compiler_params=pltpu.CompilerParams(vmem_limit_bytes=12 << 20),
    )(own, across, first)


def more_body(slots, far, beside, dense_in, dense, staged, codes, sem):
    cut = first_slots(slots)
    del dense_in

    @pl.when(in_middle())
    def _():
        col = lax.axis_index("col")
        copy = fetch_codes((far, beside), staged, codes, sem)
        copy.start()
        copy.wait()
        put_blocks(dense, far, codes, 0, cut, slots - cut, slots, col)
        put_blocks(dense, beside, codes, 1, cut, slots - cut, slots, col)


def more(far, beside, dense, slots):
    return pl.pallas_call(
        functools.partial(more_body, slots),
        out_shape=jax.ShapeDtypeStruct(dense.shape, dense.dtype),
        in_specs=spaces("v", "v", "v"),
        out_specs=spaces("v")[0],
        scratch_shapes=code_scratch(),
        input_output_aliases={2: 0},
        compiler_params=pltpu.CompilerParams(vmem_limit_bytes=12 << 20),
    )(far, beside, dense)


def multiply_groups(dense, totals, groups, codes, slots, rows):
    width = groups[0][0].shape[1]
    pieces, owners = 2, 2
    core = lax.rem(lax.axis_index("layer"), 2)
    for source in range(2):
        for slot in range(slots):
            for group, (total, packs, row) in enumerate(zip(totals, groups, rows)):
                code = codes[2 * group + source, slot]
                live = (code >= 0).astype(jnp.int32)
                safe = jnp.maximum(code, 0)
                owner = slot // (slots // owners)
                piece = lax.rem(row + owner, owners) + owners * lax.rem(safe // KB, pieces)
                inner = piece * KB + lax.rem(safe, KB)
                block_row = safe // (pieces * KB)
                sent = (lax.rem(block_row, 2) != core).astype(jnp.int32)
                spot = live * (sent * 2 + block_row // 2) + (1 - live) * 4
                part = jnp.dot(
                    packs[source][pl.ds(slot * width, width), :],
                    dense[pl.ds(pl.multiple_of(inner * width, width), width), :],
                    preferred_element_type=jnp.float32,
                )
                total[pl.ds(pl.multiple_of(spot * width, width), width), :] += part


def product_body(a_slots, slots, first_column, own_0, own_1, end_0, end_1, dense_in, first,
                 dense, keep, send, end_total, own_total, staged, codes, sem):
    cut = first_slots(slots)
    rows, columns = keep.shape[0] // 2, keep.shape[1]
    place = first_column > 0
    del dense_in

    @pl.when(jnp.logical_not(in_middle()))
    def _():
        keep[...] = jnp.zeros_like(keep)
        send[...] = jnp.zeros_like(send)

    @pl.when(in_middle())
    def _():
        copy = fetch_codes((end_0, end_1, own_0, own_1, first), staged, codes, sem)
        copy.start()
        for total in (end_total, own_total):
            total[pl.ds(0, 2 * rows), :] = jnp.zeros((2 * rows, columns), total.dtype)
        copy.wait()
        col, row = lax.axis_index("col"), lax.axis_index("row")
        if place:
            put_blocks(dense, first, codes, 4, 0, cut, slots, col)
        next_row = jnp.where(row == 1, 0, 3)
        part = dense.at[:, pl.ds(first_column, columns)]
        multiply_groups(part, (end_total, own_total), ((end_0, end_1), (own_0, own_1)), codes, a_slots, (next_row, row))
        for group, total in enumerate((end_total, own_total)):
            keep[pl.ds(group * rows, rows), :] = total[pl.ds(0, rows), :]
            send[pl.ds(group * rows, rows), :] = total[pl.ds(rows, rows), :]


def product(own, end, dense, first, first_column, columns, a_slots, slots):
    width = own[0].shape[1]
    half = jax.ShapeDtypeStruct((4 * width, columns), jnp.float32)
    return pl.pallas_call(
        functools.partial(product_body, a_slots, slots, first_column),
        out_shape=(jax.ShapeDtypeStruct(dense.shape, dense.dtype), half, half),
        in_specs=spaces(*"vvvvvv"),
        out_specs=tuple(spaces(*"vvv")),
        scratch_shapes=[pltpu.VMEM((5 * width, columns), jnp.float32)] * 2 + code_scratch(),
        input_output_aliases={4: 0},
        compiler_params=pltpu.CompilerParams(vmem_limit_bytes=20 << 20),
    )(*own, *end, dense, first)


def fold_body(keep, got, end_near, end_far, own_near, own_far):
    rows = end_near.shape[0]
    chip = lax.axis_index("layer") // 2
    extra = end_far.shape[0] - rows
    if extra:
        end_far[pl.ds(rows, extra), :] = jnp.zeros((extra, end_far.shape[1]), end_far.dtype)
    for first, near, far in ((0, end_near, end_far), (2 * rows, own_near, own_far)):
        for out, index in ((near, chip), (far, 1 - chip)):
            block = pl.ds(pl.multiple_of(first + index * rows, rows), rows)
            out[pl.ds(0, rows), :] = keep[block, :] + got[block, :]


def fold(keep, got, extra):
    rows, columns = keep.shape[0] // 4, keep.shape[1]
    part, longer = (jax.ShapeDtypeStruct((n, columns), jnp.float32) for n in (rows, rows + extra))
    return pl.pallas_call(
        fold_body,
        out_shape=(part, longer, part, part),
        in_specs=spaces(*"vv"),
        out_specs=tuple(spaces(*"vvvv")),
        compiler_params=pltpu.CompilerParams(vmem_limit_bytes=8 << 20),
    )(keep, got)


def settle_body(near, got, out):
    out[...] = (near[...] + got[...]).astype(out.dtype)


def settle(near, got):
    return pl.pallas_call(
        settle_body,
        out_shape=jax.ShapeDtypeStruct(near.shape, jnp.bfloat16),
        in_specs=spaces("v", "v"),
        out_specs=spaces("v")[0],
        compiler_params=pltpu.CompilerParams(vmem_limit_bytes=4 << 20),
    )(near, got)


def finish_body(left, left_got, right, right_got, near, far, settled, out):
    cut = left.shape[1]
    out[:, pl.ds(0, cut)] = ((left[...] + left_got[...]) + (near[...] + far[pl.ds(0, near.shape[0]), :])).astype(out.dtype)
    rest = (right[...] + right_got[...]) + settled[...].astype(jnp.float32)
    out[:, pl.ds(cut, rest.shape[1])] = rest.astype(out.dtype)


def finish(*parts):
    shape = (parts[0].shape[0], parts[0].shape[1] + parts[2].shape[1])
    return pl.pallas_call(
        finish_body,
        out_shape=jax.ShapeDtypeStruct(shape, jnp.bfloat16),
        in_specs=spaces(*"vvvvvvv"),
        out_specs=spaces("v")[0],
        compiler_params=pltpu.CompilerParams(vmem_limit_bytes=4 << 20),
    )(*parts)


BESIDE = [(0, 1), (1, 0), (2, 3), (3, 2)]
BEYOND = [(0, 2), (2, 3), (3, 1), (1, 0)]
COLS = [(0, 1), (1, 0)]
CORES = [(0, 1), (1, 0), (2, 3), (3, 2)]
EVERY = [(r, m) for r in range(4) for m in range(4)]
MIDDLE = [(r * 4 + m, (3 - r) * 4 + m if r in (1, 2) else r * 4 + (m ^ 1)) for r, m in EVERY]
CHIPS = [(r * 4 + m, r * 4 + (m ^ 2 if r in (1, 2) else m ^ 1)) for r, m in EVERY]
ACROSS = [(r * 4 + m, (r ^ 1) * 4 + (m ^ 2 if r in (1, 2) else m)) for r, m in EVERY]


def middle_shards(a_blocks, a_codes, b_blocks, b_codes):
    a_slots, slots = a_blocks.shape[0], b_blocks.shape[0]
    a_pack, b_pack, mixed, b_second = pack(a_codes, b_codes, a_blocks, b_blocks)
    b_across = lax.ppermute(b_pack, ("row", "layer"), MIDDLE)
    end_mixed = lax.ppermute(mixed, "row", BESIDE)
    far_second = lax.ppermute(b_second, "row", BEYOND)
    a_other = lax.ppermute(a_pack, "col", COLS)
    b_late, a_other = lax.optimization_barrier((b_second, a_other))
    end_second = lax.ppermute(b_late, "row", BESIDE)
    end_first, a_end = part(end_mixed, end_mixed.shape[0] - a_pack.shape[0])
    far_first = lax.ppermute(end_first, ("row", "layer"), MIDDLE)
    a_end, a_other = lax.optimization_barrier((a_end, a_other))
    a_end_other = lax.ppermute(a_end, "col", COLS)

    dense = early(b_pack, b_across, end_first, slots)
    columns = CB * a_blocks.shape[1]
    cut = columns * CUT // 4
    own, end = (a_pack, a_other), (a_end, a_end_other)
    dense = more(far_second, end_second, dense, slots)
    dense, keep, send = product(own, end, dense, far_first, cut, columns - cut, a_slots, slots)
    got = lax.ppermute(send, "layer", CORES)
    _, left_keep, left_send = product(own, end, dense, far_first, 0, cut, a_slots, slots)
    left_got = lax.ppermute(left_send, "layer", CORES)
    rest_near, rest_far, right, right_far = fold(keep, got, 0)
    rest_got = lax.ppermute(rest_far, ("row", "layer"), CHIPS)
    settled = lax.ppermute(settle(rest_near, rest_got), "row", BESIDE)
    right_got = lax.ppermute(right_far, ("row", "layer"), CHIPS)
    near, far, left, left_far = fold(left_keep, left_got, 8)
    got_near = lax.ppermute(near, "row", BESIDE)
    got_far = lax.ppermute(far, ("row", "layer"), ACROSS)
    left_got = lax.ppermute(left_far, ("row", "layer"), CHIPS)
    return finish(left, left_got, right, right_got, got_near, got_far, settled)


def solution(mesh):
    placed = (
        P(("row", "col", "layer"), None, None),
        P(("row", "col", "layer")),
        P(("row", "col", "layer"), None, None),
        P(("row", "col", "layer")),
    )
    body = middle_shards if middle_plan(mesh.shape) else shards
    return jax.shard_map(
        body, mesh=mesh, in_specs=placed, out_specs=P(("row", "layer"), "col"), check_vma=False
    )
```
